128 devices in a mesh: row: 8 (over y, core), col: 16 (over x, z).
Axes of the slice: x: 4, y: 4, z: 4, core: 2. Of those that a mesh axis runs over, the one named last changes fastest.
Arguments:
- image: bfloat16 [64, 256, 128], P('row', 'col'), may hold values from -6 to 6
- in_weight: bfloat16 [128, 512], replicated, may hold values from -0.5 to 0.5
- conv_weight: float32 [3, 3, 256], replicated, may hold values from -2 to 2
- conv_bias: float32 [256], replicated, may hold values from -3 to 3
- proj_weight: float32 [4, 256, 40], replicated, may hold values from -0.375 to 0.375
- dt_weight: float32 [4, 8, 256], replicated, may hold values from -2 to 2
- dt_bias: float32 [4, 256], replicated, may hold values from -1 to 1
- a_log: float32 [4, 16, 256], replicated, may hold values from -8 to -2, as said below
- skip_gain: float32 [4, 256], replicated, may hold values from 0.5 to 1.5
- norm_gain: float32 [256], replicated, may hold values from 0.1 to 1.9
- out_weight: bfloat16 [256, 128], replicated, may hold values from -0.375 to 0.375
- cotangent: bfloat16 [64, 256, 128], P('row', 'col'), may hold values from -6 to 6
Outputs:
- block_out: bfloat16 [64, 256, 128], P('row', 'col')
- grad_image: bfloat16 [64, 256, 128], P('row', 'col')
- grad_in_weight: float32 [128, 512], replicated
- grad_out_weight: float32 [256, 128], replicated
- grad_a_log: float32 [4, 16, 256], replicated
The draws below stay inside these ranges and needn't reach their ends.
Inputs may be any that keep to these rules, and one draw needn't show every extreme that they name: `a_log`: entries of direction k lie between log(0.2 / L) and -2, with L the tokens of one line of that direction (256 for directions 0 and 1, 64 for 2 and 3).
All inputs are finite; a program needn't handle non-finite values.
Results may differ from the reference program's by a relative error of at most 0.0019.
Values sent between devices are 32-bit elements; how exact they have to be, the bound alone decides.
No kernel may reach another device: no remote copies, remote signals or barrier semaphores. Data moves between devices by JAX's collectives and lax.ppermute only.
A program may use at most 128 MiB of HBM per device.

```python
import jax
import jax.numpy as jnp
from jax import lax

WIDTH = 128
INNER = 256
STATE = 16
DT_RANK = 8
PROJ = 40
GRID_ROWS = 64
GRID_COLS = 256


def draw_a_log(key, part):
    key = jax.random.fold_in(key, 7)
    lengths = jnp.array([GRID_COLS, GRID_COLS, GRID_ROWS, GRID_ROWS], jnp.float32)[:, None, None]
    lowest = jnp.log(0.2 / lengths)
    highest_log = jnp.log(jnp.full_like(lengths, 0.1))
    fraction = jax.random.uniform(key, (4, STATE, INNER), jnp.float32)
    return (lowest + (highest_log - lowest) * fraction).astype(jnp.float32)


def steps_of(rng, dims, split, low, top_value):
    loudness = 1.0
    for dim, parts in split:
        draws = jax.random.uniform(jax.random.fold_in(jax.random.fold_in(rng, 6), dim), (parts,), jnp.float32, low / len(split), top_value / len(split))
        loudness = loudness * jnp.repeat(jnp.exp(draws), dims[dim] // parts).reshape((-1,) + (1,) * (len(dims) - 1 - dim))
    return loudness


def centred(stream_key, dims, deviation, reach, split=(), kind=jnp.bfloat16):
    values = jax.random.normal(stream_key, dims, jnp.float32) * deviation
    if len(split) > 0:
        values = steps_of(stream_key, dims, split, -0.22, 0.18) * values
    return jnp.clip(values, min=-reach, max=reach).astype(kind)


def setup_inputs(seed: int = 0) -> dict:
    splits = jax.random.split(jax.random.key(seed), 13)
    image = centred(splits[0], (GRID_ROWS, GRID_COLS, WIDTH), 1.0, 6.0, ((0, 8), (1, 16)))
    in_weight = centred(splits[1], (WIDTH, 2 * INNER), WIDTH ** -0.5, 0.5)
    conv_weight = centred(splits[2], (3, 3, INNER), 9 ** -0.5, 2.0, (), jnp.float32)
    conv_bias = centred(splits[3], (INNER,), 0.5, 3.0, (), jnp.float32)
    proj_weight = centred(splits[4], (4, INNER, PROJ), INNER ** -0.5, 0.375, (), jnp.float32)
    dt_weight = centred(splits[5], (4, DT_RANK, INNER), DT_RANK ** -0.5, 2.0, (), jnp.float32)
    dt_bias = jnp.clip(jax.random.uniform(splits[6], (4, INNER), jnp.float32, -1.0, 1.0), -1.0, 1.0)
    a_log = draw_a_log(jax.random.fold_in(splits[12], 71), 0)
    skip_gain = jnp.clip(jax.random.uniform(splits[8], (4, INNER), jnp.float32, 0.5, 1.5), 0.5, 1.5)
    norm_gain = jnp.clip(1.0 + 0.18 * jax.random.normal(splits[9], (INNER,), jnp.float32), 0.1, 1.9)
    out_weight = centred(splits[10], (INNER, WIDTH), INNER ** -0.5, 0.375)
    cotangent = centred(splits[11], (GRID_ROWS, GRID_COLS, WIDTH), 1.0, 6.0, ((0, 8), (1, 16)))
    return dict(image=image, in_weight=in_weight, conv_weight=conv_weight, conv_bias=conv_bias, proj_weight=proj_weight, dt_weight=dt_weight, dt_bias=dt_bias, a_log=a_log, skip_gain=skip_gain, norm_gain=norm_gain, out_weight=out_weight, cotangent=cotangent)


def line_scan(inputs, proj_w, dt_w, dt_b, a_values, skip, start):
    project = jnp.einsum('lte,ef->ltf', inputs, proj_w, precision=lax.Precision.HIGHEST)
    low_rank = project[..., :DT_RANK]
    entry = project[..., DT_RANK:DT_RANK + STATE]
    readout = project[..., DT_RANK + STATE:]
    delta = jax.nn.softplus(jnp.einsum('ltr,re->lte', low_rank, dt_w, precision=lax.Precision.HIGHEST) + dt_b)
    rates = -jnp.exp(a_values)

    def advance(state, item):
        delta_now, entry_now, readout_now, input_now = item
        state = jnp.exp(delta_now[:, None, :] * rates) * state + (delta_now * input_now)[:, None, :] * entry_now[:, :, None]
        return (state, lax.optimization_barrier(jnp.sum(readout_now[:, :, None] * state, axis=1)))
    items = tuple((jnp.swapaxes(value, 0, 1) for value in (delta, entry, readout, inputs)))
    final, outputs = lax.scan(advance, start, items)
    decay = jnp.exp(rates * lax.optimization_barrier(jnp.sum(delta, axis=1))[:, None, :])
    return (jnp.swapaxes(outputs, 0, 1) + skip * inputs, final, decay)

def orient(field, direction):
    if direction == 0:
        return field
    if direction == 1:
        return jnp.flip(field, 1)
    if direction == 2:
        return jnp.swapaxes(field, 0, 1)
    return jnp.flip(jnp.swapaxes(field, 0, 1), 1)

def restore(field, direction):
    if direction == 0:
        return field
    if direction == 1:
        return jnp.flip(field, 1)
    if direction == 2:
        return jnp.swapaxes(field, 0, 1)
    return jnp.swapaxes(jnp.flip(field, 1), 0, 1)

def mixer(padded, gate_in, conv_weight, conv_bias, proj_weight, dt_weight, dt_bias, a_values, skip_gain, norm_gain, out_matrix, starts):
    height = gate_in.shape[0]
    span = gate_in.shape[1]
    conv = conv_bias + jnp.zeros_like(gate_in)
    for offset_row in range(3):
        for offset_col in range(3):
            conv = conv + padded[offset_row:offset_row + height, offset_col:offset_col + span] * conv_weight[offset_row, offset_col]
    hidden = jax.nn.silu(conv)
    total = jnp.zeros_like(hidden)
    finals = []
    decays = []
    for direction in range(4):
        result, final, decay = jax.checkpoint(line_scan)(orient(hidden, direction), proj_weight[direction], dt_weight[direction], dt_bias[direction], a_values[direction], skip_gain[direction], starts[direction])
        total = total + restore(result, direction)
        finals.append(final)
        decays.append(decay)
    center = lax.optimization_barrier(jnp.mean(total, axis=-1, keepdims=True))
    centered = total - center
    spread = lax.optimization_barrier(jnp.mean(centered * centered, axis=-1, keepdims=True))
    normed = centered * lax.rsqrt(spread + 1e-05) * norm_gain
    gated = normed * jax.nn.silu(gate_in)
    out = jnp.einsum('hwe,ec->hwc', gated, out_matrix, precision=lax.Precision.HIGHEST)
    return ((out, tuple(finals)), tuple(decays))

def reference(image, in_weight, conv_weight, conv_bias, proj_weight, dt_weight, dt_bias, a_log, skip_gain, norm_gain, out_weight, cotangent):
    mixed = jnp.einsum('hwc,cf->hwf', image, in_weight, preferred_element_type=jnp.float32)

    def forward(mixed_in, a_values, out_matrix):
        padded = jnp.pad(mixed_in[..., :INNER], ((1, 1), (1, 1), (0, 0)))
        row_zero = jnp.zeros((GRID_ROWS, STATE, INNER), jnp.float32)
        col_zero = jnp.zeros((GRID_COLS, STATE, INNER), jnp.float32)
        starts = (row_zero, row_zero, col_zero, col_zero)
        (out, finals), decays = mixer(padded, mixed_in[..., INNER:], conv_weight, conv_bias, proj_weight, dt_weight, dt_bias, a_values, skip_gain, norm_gain, out_matrix, starts)
        return out
    out, pullback = jax.vjp(forward, mixed, a_log, out_weight.astype(jnp.float32))
    grad_mixed, grad_a, grad_out = pullback(cotangent.astype(jnp.float32))
    flat_grad = grad_mixed.reshape(GRID_ROWS * GRID_COLS, 2 * INNER)
    grad_pixels = jnp.dot(flat_grad, in_weight.astype(jnp.float32).T, precision=lax.Precision.HIGHEST).reshape(GRID_ROWS, GRID_COLS, WIDTH)
    flat_pixels = image.astype(jnp.float32).reshape(GRID_ROWS * GRID_COLS, WIDTH)
    grad_in = jnp.dot(flat_pixels.T, flat_grad, precision=lax.Precision.HIGHEST)
    return (out.astype(jnp.bfloat16), grad_pixels.astype(jnp.bfloat16), grad_in, grad_out, grad_a)
```

```python
from functools import partial

import jax
import jax.numpy as jnp
from jax import lax
from jax.experimental import pallas as pl
from jax.experimental.pallas import tpu as pltpu
from jax.sharding import PartitionSpec as P

F32 = jnp.float32
BF16 = jnp.bfloat16
H, W, C, E, N = 8, 16, 128, 256, 16
LOG2E = 1.4426950408889634
LN2 = 0.6931471805599453
AXES = ("row", "col")


def split2(a):
    hi = a.astype(BF16)
    return hi, (a - hi.astype(F32)).astype(BF16)


def dot(a, b, dims):
    return lax.dot_general(a, b, (dims, ((), ())), preferred_element_type=F32)


NN = ((1,), (0,))
NT = ((1,), (1,))


def mm3(a, b, dims=NN):
    ah, al = split2(a)
    bh, bl = split2(b)
    return dot(ah, bh, dims) + (dot(ah, bl, dims) + dot(al, bh, dims))


def mm2(a, b, dims=NN):
    ah, al = split2(a)
    return dot(ah, b, dims) + dot(al, b, dims)


def mm2r(a, b, dims=NN):
    bh, bl = split2(b)
    return dot(a, bh, dims) + dot(a, bl, dims)


def permute_tokens(x, to_cr):
    o = lax.broadcasted_iota(jnp.int32, (128, 128), 0)
    i = lax.broadcasted_iota(jnp.int32, (128, 128), 1)
    if to_cr:
        hit = i == ((o & 7) * 16 + (o >> 3))
    else:
        hit = i == ((o & 15) * 8 + (o >> 4))
    m = jnp.where(hit, 1.0, 0.0).astype(BF16)
    hi = x.astype(BF16)
    rest = x - hi.astype(F32)
    mid = rest.astype(BF16)
    low = (rest - mid.astype(F32)).astype(BF16)
    return dot(m, hi, NN) + (dot(m, mid, NN) + dot(m, low, NN))


def softplus(z):
    return jnp.maximum(z, 0.0) + jnp.log1p(jnp.exp(-jnp.abs(z)))


def sigmoid(v):
    return 1.0 / (1.0 + jnp.exp(-v))


def lanes(v, lane):
    return jnp.broadcast_to(v[:, lane : lane + 1], (8, E))


def fill_rates(alog, rate):
    r = -jnp.exp(alog[...]) * LOG2E
    for i in range(4 * N):
        rate[i] = jnp.broadcast_to(r[i : i + 1], (8, E))


def steps(k):
    return W if k < 2 else H


def groups(k):
    return (0,) if k < 2 else (0, 1)


def row_at(k, g, i):
    t = i if k % 2 == 0 else steps(k) - 1 - i
    start = t * 8 if k < 2 else t * 16 + g * 8
    return pl.multiple_of(start, 8)


def send_layout(pos, col_f, col_d, row_f, row_d, mz, mc):
    z, core = pos[0], pos[3]
    for d in range(4):
        q = jnp.bitwise_xor(z, d)
        for f in range(2):
            mz[d][f, 0:4] = col_f[f, pl.ds(4 * q, 4)]
            mz[d][f, 4] = col_d[f]
    for d in range(2):
        h = jnp.bitwise_xor(core, d)
        for f in range(2):
            mc[d][f, 0:8] = row_f[f, pl.ds(8 * h, 8)]
            mc[d][f, 8] = row_d[f]


def first_kernel(
    pos, pix, img, win, cw, cb, p01w, p23w, dtw, dtb, alog,
    hid_rc, hid_cr, conv, gate, z, p01, p23, mz0, mz1, mz2, mz3, mc0, mc1,
    rate, delta, mix, col_f, col_d, row_f, row_d,
):
    fill_rates(alog, rate)
    x = pix[...].reshape(10 * 24, C).astype(BF16)
    mix[...] = dot(x, win[:, :E], NN).reshape(10, 24, E)
    gate[...] = dot(img[...], win[:, E:], NN)
    acc = jnp.broadcast_to(cb[...].reshape(1, 1, E), (H, W, E))
    for j in range(3):
        for i in range(3):
            acc = acc + mix[i : i + H, j : j + W, :] * cw[3 * i + j].reshape(1, 1, E)
    acc = acc.reshape(H * W, E)
    conv[...] = acc
    hid = acc * sigmoid(acc)
    hid_rc[...] = hid
    cr = permute_tokens(hid, True)
    hid_cr[...] = cr
    p01[...] = mm3(cr, p01w[...])
    p23[...] = mm3(hid, p23w[...])
    for k in range(4):
        zk = mm3((p01 if k < 2 else p23)[...], dtw[k]) + dtb[k]
        z[k] = zk
        delta[k] = softplus(zk)
    for k in range(4):
        p, h = (p01, hid_cr) if k < 2 else (p23, hid_rc)
        base = 40 * (k % 2) + 8
        for g in groups(k):

            def body(i, s, k=k, g=g, p=p, h=h, base=base):
                at = pl.ds(row_at(k, g, i), 8)
                d = delta[k, at, :]
                u = d * h[at, :]
                b = p[at, :]
                new = [
                    jnp.exp2(d * rate[k * N + n]) * s[n] + u * lanes(b, base + n)
                    for n in range(N)
                ]
                return tuple(new) + (s[N] + d,)

            zero = jnp.zeros((8, E), F32)
            s = lax.fori_loop(0, steps(k), body, (zero,) * (N + 1))
            f = k % 2
            if k < 2:
                for n in range(N):
                    col_f[f, n] = s[n]
                col_d[f] = s[N]
            else:
                for n in range(N):
                    row_f[f, n, 8 * g : 8 * g + 8, :] = s[n]
                row_d[f, 8 * g : 8 * g + 8, :] = s[N]
    send_layout(pos, col_f, col_d, row_f, row_d, (mz0, mz1, mz2, mz3), (mc0, mc1))


def decay(alog, k, n, d):
    r = -jnp.exp(alog[k, n]) * LOG2E
    return jnp.exp2(d * jnp.broadcast_to(r, d.shape))


def join_kernel(ks, pos, alog, r0, r1, r2, r3, c0, c1, mx1, mx2, mx3, my1, my2, my3, rs, rc, gx, gy):
    z, x, y, core = pos[0], pos[1], pos[2], pos[3]
    for d, r in enumerate((r0, r1, r2, r3)):
        rs[jnp.bitwise_xor(z, d)] = r[...]
    for d, r in enumerate((c0, c1)):
        rc[jnp.bitwise_xor(core, d)] = r[...]
    for f in range(2):
        order = range(4) if f == 0 else range(3, -1, -1)
        for n in range(4):
            total = None
            for t in order:
                piece = rs[t, f, n]
                total = piece if total is None else (
                    total * decay(alog, ks[f], 4 * z + n, rs[t, f, 4]) + piece
                )
            gx[f, n] = total
        gx[f, 4] = rs[0, f, 4] + rs[1, f, 4] + rs[2, f, 4] + rs[3, f, 4]
        one, two = (0, 1) if f == 0 else (1, 0)
        for n in range(8):
            gy[f, n] = (
                rc[one, f, n] * decay(alog, ks[2 + f], 8 * core + n, rc[two, f, 8])
                + rc[two, f, n]
            )
        gy[f, 8] = rc[0, f, 8] + rc[1, f, 8]
    for d, m in ((1, mx1), (2, mx2), (3, mx3)):
        m[...] = gx[jnp.where(jnp.bitwise_xor(x, d) > x, 0, 1)]
    for d, m in ((1, my1), (2, my2), (3, my3)):
        m[...] = gy[jnp.where(jnp.bitwise_xor(y, d) > y, 0, 1)]


def start_kernel(
    ks, pos, alog, r0, r1, r2, r3, c0, c1, x1, x2, x3, y1, y2, y3,
    so0, so1, so2, so3, co0, co1, rs, rc, xs, ys, oz, oc,
):
    z, x, y, core = pos[0], pos[1], pos[2], pos[3]
    for d, r in enumerate((r0, r1, r2, r3)):
        rs[jnp.bitwise_xor(z, d)] = r[...]
    for d, r in enumerate((c0, c1)):
        rc[jnp.bitwise_xor(core, d)] = r[...]
    xs[x] = jnp.zeros((5, 8, E), F32)
    ys[y] = jnp.zeros((9, 16, E), F32)
    for d, r in ((1, x1), (2, x2), (3, x3)):
        xs[jnp.bitwise_xor(x, d)] = r[...]
    for d, r in ((1, y1), (2, y2), (3, y3)):
        ys[jnp.bitwise_xor(y, d)] = r[...]
    for f in range(2):
        order = list(range(4)) if f == 0 else list(range(3, -1, -1))
        for n in range(4):
            s = jnp.zeros((8, E), F32)
            for p in order:
                before = p < x if f == 0 else p > x
                new = s * decay(alog, ks[f], 4 * z + n, xs[p, 4]) + xs[p, n]
                s = jnp.where(before, new, s)
            for t in order:
                oz[t, f, n] = s
                if t != order[-1]:
                    s = s * decay(alog, ks[f], 4 * z + n, rs[t, f, 4]) + rs[t, f, n]
        one, two = (0, 1) if f == 0 else (1, 0)
        for n in range(8):
            s = jnp.zeros((16, E), F32)
            for p in order:
                before = p < y if f == 0 else p > y
                new = s * decay(alog, ks[2 + f], 8 * core + n, ys[p, 8]) + ys[p, n]
                s = jnp.where(before, new, s)
            oc[one, f, n] = s
            oc[two, f, n] = (
                s * decay(alog, ks[2 + f], 8 * core + n, rc[one, f, 8]) + rc[one, f, n]
            )
    for d, o in enumerate((so0, so1, so2, so3)):
        o[...] = oz[jnp.bitwise_xor(z, d)]
    for d, o in enumerate((co0, co1)):
        o[...] = oc[jnp.bitwise_xor(core, d)]


def place_starts(pos, t, u, col_s, row_s):
    z, core = pos[0], pos[3]
    for d in range(4):
        q = jnp.bitwise_xor(z, d)
        for f in range(2):
            col_s[f, pl.ds(4 * q, 4)] = t[d][f]
    for d in range(2):
        h = jnp.bitwise_xor(core, d)
        for f in range(2):
            row_s[f, pl.ds(8 * h, 8)] = u[d][f]


def start_of(k, g, n, col_s, row_s, flip):
    f = (k % 2) ^ flip
    return col_s[f, n] if k < 2 else row_s[f, n, 8 * g : 8 * g + 8, :]


def middle_kernel(
    pos, t0, t1, t2, t3, u0, u1, hid_rc, hid_cr, gate, z, p01, p23, alog, skip, gain,
    ow, win, cot, img,
    out, g_out, g_gate, gate_pix, dtot_rc, dtot_cr, mz0, mz1, mz2, mz3, mc0, mc1,
    rate, delta, y01, y23, col_s, row_s, col_d, row_d,
):
    fill_rates(alog, rate)
    place_starts(pos, (t0, t1, t2, t3), (u0, u1), col_s, row_s)
    for k in range(4):
        delta[k] = softplus(z[k])
    for k in range(4):
        p, h, yy = (p01, hid_cr, y01) if k < 2 else (p23, hid_rc, y23)
        base = 40 * (k % 2) + 8
        for g in groups(k):

            def body(i, s, k=k, g=g, p=p, h=h, yy=yy, base=base):
                at = pl.ds(row_at(k, g, i), 8)
                d = delta[k, at, :]
                u = d * h[at, :]
                b = p[at, :]
                y = None
                new = []
                for n in range(N):
                    v = jnp.exp2(d * rate[k * N + n]) * s[n] + u * lanes(b, base + n)
                    new.append(v)
                    c = v * lanes(b, base + N + n)
                    y = c if y is None else y + c
                yy[at, :] = y if k % 2 == 0 else yy[at, :] + y
                return tuple(new)

            s = tuple(start_of(k, g, n, col_s, row_s, 0) for n in range(N))
            lax.fori_loop(0, steps(k), body, s)
    skips = skip[0:1] + skip[1:2] + skip[2:3] + skip[3:4]
    total = y23[...] + permute_tokens(y01[...], False) + skips * hid_rc[...]
    centered = total - jnp.mean(total, axis=-1, keepdims=True)
    inv = lax.rsqrt(jnp.mean(centered * centered, axis=-1, keepdims=True) + 1e-05)
    unit = centered * inv
    normed = unit * gain[...]
    gv = gate[...]
    sg = sigmoid(gv)
    act = gv * sg
    gated = normed * act
    out[...] = mm2(gated, ow[...]).astype(BF16)
    g_out[...] = mm2(gated.T, cot[...])
    dgated = dot(cot[...], ow[...], NT)
    dgate = dgated * normed * (sg * (1.0 + gv * (1.0 - sg)))
    imt = img[...].astype(F32).T.astype(BF16)
    g_gate[...] = mm2r(imt, dgate)
    gate_pix[...] = mm2(dgate, win[:, E:], NT)
    dn = dgated * act * gain[...]
    dt = inv * (
        dn
        - jnp.mean(dn, axis=-1, keepdims=True)
        - unit * jnp.mean(dn * unit, axis=-1, keepdims=True)
    )
    dtot_rc[...] = dt
    dtot_cr[...] = permute_tokens(dt, True)
    for k in range(4):
        p, dy = (p01, dtot_cr) if k < 2 else (p23, dtot_rc)
        base = 40 * (k % 2) + 8 + N
        f = 1 - k % 2
        for g in groups(k):

            def back(i, s, k=k, g=g, p=p, dy=dy, base=base):
                at = pl.ds(row_at(k, g, steps(k) - 1 - i), 8)
                d = delta[k, at, :]
                b = p[at, :]
                t = dy[at, :]
                new = [
                    jnp.exp2(d * rate[k * N + n]) * (s[n] + t * lanes(b, base + n))
                    for n in range(N)
                ]
                return tuple(new) + (s[N] + d,)

            zero = jnp.zeros((8, E), F32)
            s = lax.fori_loop(0, steps(k), back, (zero,) * (N + 1))
            if k < 2:
                for n in range(N):
                    col_s[f, n] = s[n]
                col_d[f] = s[N]
            else:
                for n in range(N):
                    row_s[f, n, 8 * g : 8 * g + 8, :] = s[n]
                row_d[f, 8 * g : 8 * g + 8, :] = s[N]
    send_layout(pos, col_s, col_d, row_s, row_d, (mz0, mz1, mz2, mz3), (mc0, mc1))


def last_kernel(
    pos, t0, t1, t2, t3, u0, u1, b0, b1, b2, b3, v0, v1,
    hid_rc, hid_cr, conv, z, p01, p23, dtot_rc, dtot_cr, alog, skip,
    p01w, p23w, dtw, cw, win, pix, g_out, g_gate, gate_pix,
    msg, center,
    rate, delta, col_s, row_s, col_b, row_b, hist, drate, dx01, dx23, dp01, dp23, dz,
    zpad, gp, edge,
):
    fill_rates(alog, rate)
    place_starts(pos, (t0, t1, t2, t3), (u0, u1), col_s, row_s)
    place_starts(pos, (b0, b1, b2, b3), (v0, v1), col_b, row_b)
    lane = lax.broadcasted_iota(jnp.int32, (8, 128), 1)
    for k in range(4):
        delta[k] = softplus(z[k])
    drate[...] = jnp.zeros_like(drate)
    for k in range(4):
        p, h, dy, dx, dp = (
            (p01, hid_cr, dtot_cr, dx01, dp01) if k < 2 else (p23, hid_rc, dtot_rc, dx23, dp23)
        )
        base = 40 * (k % 2) + 8
        last = steps(k)
        for g in groups(k):

            def body(i, s, k=k, g=g, p=p, h=h, base=base):
                at = pl.ds(row_at(k, g, i), 8)
                d = delta[k, at, :]
                u = d * h[at, :]
                b = p[at, :]
                new = []
                for n in range(N):
                    hist[i, n] = s[n]
                    new.append(
                        jnp.exp2(d * rate[k * N + n]) * s[n] + u * lanes(b, base + n)
                    )
                return tuple(new)

            s = tuple(start_of(k, g, n, col_s, row_s, 0) for n in range(N))
            s = lax.fori_loop(0, last, body, s)
            for n in range(N):
                hist[last, n] = s[n]

            def back(j, m, k=k, g=g, p=p, h=h, dy=dy, dx=dx, dp=dp, base=base, last=last):
                i = last - 1 - j
                at = pl.ds(row_at(k, g, i), 8)
                d = delta[k, at, :]
                xx = h[at, :]
                u = d * xx
                b = p[at, :]
                t = dy[at, :]
                row = jnp.zeros((8, 128), F32)
                du = jnp.zeros((8, E), F32)
                dd = jnp.zeros((8, E), F32)
                new = []
                for n in range(N):
                    r = rate[k * N + n]
                    lam = lanes(b, base + N + n) * t + m[n]
                    out = jnp.exp2(d * r) * lam
                    new.append(out)
                    dc = jnp.sum(t * hist[i + 1, n], axis=-1, keepdims=True)
                    db = jnp.sum(lam * u, axis=-1, keepdims=True)
                    row = jnp.where(lane == base + n, db, row)
                    row = jnp.where(lane == base + N + n, dc, row)
                    du = du + lam * lanes(b, base + n)
                    q = out * hist[i, n]
                    dd = dd + q * r
                    drate[k * N + n] = drate[k * N + n] + q * d
                ddel = du * xx + dd * LN2
                dz[k, at, :] = ddel * sigmoid(z[k, at, :])
                dxv = du * d + skip[k : k + 1] * t
                if k % 2 == 0:
                    dx[at, :] = dxv
                    dp[at, :] = row
                else:
                    dx[at, :] = dx[at, :] + dxv
                    dp[at, :] = dp[at, :] + row
                return tuple(new)

            m = tuple(start_of(k, g, n, col_b, row_b, 1) for n in range(N))
            lax.fori_loop(0, last, back, m)
    g_a = jnp.sum(drate[...], axis=1) * (-jnp.exp(alog[...]))
    d01 = dp01[...] + mm3(dz[0], dtw[0], NT) + mm3(dz[1], dtw[1], NT)
    d23 = dp23[...] + mm3(dz[2], dtw[2], NT) + mm3(dz[3], dtw[3], NT)
    dcr = dx01[...] + mm3(d01, p01w[...], NT)
    drc = dx23[...] + mm3(d23, p23w[...], NT)
    dhid = drc + permute_tokens(dcr, False)
    cv = conv[...]
    sg = sigmoid(cv)
    dconv = dhid * (sg * (1.0 + cv * (1.0 - sg)))
    zpad[...] = jnp.zeros_like(zpad)
    zpad[2:10, 8:24, :] = dconv.reshape(H, W, E)
    acc = jnp.zeros((10, 24, E), F32)
    for j in range(3):
        for i in range(3):
            acc = acc + zpad[2 - i : 12 - i, 8 - j : 32 - j, :] * cw[3 * i + j].reshape(1, 1, E)
    flat = acc.reshape(240, E)
    gp[...] = mm2(flat, win[:, :E], NT).reshape(10, 24, C)
    pt = pix[...].reshape(240, C)
    g_in = mm2r(pt.T.astype(BF16), flat)
    center[...] = gate_pix[...] + gp[1:9, 1:17, :].reshape(128, C)
    edge[...] = jnp.zeros_like(edge)
    edge[0:16] = gp[9, 1:17, :]
    edge[16:32] = gp[0, 1:17, :]
    edge[32:40] = gp[1:9, 17, :]
    edge[40:48] = gp[1:9, 0, :]
    edge[48:49] = gp[9, 17:18, :]
    edge[49:50] = gp[9, 0:1, :]
    edge[50:51] = gp[0, 17:18, :]
    edge[51:52] = gp[0, 0:1, :]
    blocks = (
        g_in[:, :128],
        g_in[:, 128:],
        g_gate[:, :128],
        g_gate[:, 128:],
        g_out[:128],
        g_out[128:],
        jnp.concatenate([g_a[:, :128], g_a[:, 128:]], axis=0),
        edge[...].T,
    )
    for b, block in enumerate(blocks):
        msg[pl.ds(b, 128, stride=8), :] = block


def sum_kernel(r, o):
    s = jnp.sum(r[...].reshape(128, 8, 128), axis=0)
    h = r[pl.ds(7, 128, stride=8), :]
    d = lax.broadcasted_iota(jnp.int32, (128, 128), 0)
    i = lax.broadcasted_iota(jnp.int32, (128, 128), 1)
    rr, cc = d >> 4, d & 15
    inn = jnp.zeros((128, 128), F32)
    for lo, hi, dr, dc in (
        (0, 16, -1, 0), (16, 32, 1, 0), (32, 40, 0, -1), (40, 48, 0, 1),
        (48, 49, -1, -1), (49, 50, -1, 1), (50, 51, 1, -1), (51, 52, 1, 1),
    ):
        moved = pltpu.roll(h, (-(dr * 16 + dc)) % 128, 0)
        ok = (i >= lo) & (i < hi)
        ok = ok & (rr + dr >= 0) & (rr + dr < 8) & (cc + dc >= 0) & (cc + dc < 16)
        inn = jnp.where(ok, moved, inn)
    o[...] = jnp.broadcast_to(s[None], (128, 8, 128)).reshape(1024, 128)
    o[pl.ds(7, 128, stride=8), :] = inn


def finish_kernel(q, center, g_pix, g_in, g_out, g_a, acc):
    def block(b):
        return q[pl.ds(b, 128, stride=8), :]

    for b in range(4):
        g_in[:, 128 * b : 128 * b + 128] = block(b)
    g_out[:128] = block(4)
    g_out[128:] = block(5)
    a = block(6)
    g_a[:, :128] = a[:64]
    g_a[:, 128:] = a[64:]
    inn = block(7).T
    acc[...] = center[...].reshape(H, W, C)
    acc[0] = acc[0] + inn[0:16]
    acc[7] = acc[7] + inn[16:32]
    acc[:, 0, :] = acc[:, 0, :] + inn[32:40]
    acc[:, 15, :] = acc[:, 15, :] + inn[40:48]
    acc[0, 0:1, :] = acc[0, 0:1, :] + inn[48:49]
    acc[0, 15:16, :] = acc[0, 15:16, :] + inn[49:50]
    acc[7, 0:1, :] = acc[7, 0:1, :] + inn[50:51]
    acc[7, 15:16, :] = acc[7, 15:16, :] + inn[51:52]
    g_pix[...] = acc[...].reshape(H * W, C).astype(BF16)


def call(kernel, ins, outs, scratch, name):
    vmem = pl.BlockSpec(memory_space=pltpu.VMEM)
    specs = [
        pl.BlockSpec(memory_space=pltpu.SMEM) if x.dtype == jnp.int32 else vmem for x in ins
    ]
    return pl.pallas_call(
        kernel,
        out_shape=[jax.ShapeDtypeStruct(s, t) for s, t in outs],
        in_specs=specs,
        out_specs=[vmem] * len(outs),
        scratch_shapes=[pltpu.VMEM(s, F32) for s in scratch],
        compiler_params=pltpu.CompilerParams(vmem_limit_bytes=44 * 1024 * 1024),
        name=name,
    )(*ins)


def xor_permute(x, axis, mask):
    return lax.ppermute(x, axis, [(i, i ^ mask) for i in range(lax.axis_size(axis))])


def exchange(pos, alog4, mz, mc, ks):
    c = [mc[0], xor_permute(mc[1], "row", 1)]
    r = [mz[0]] + [xor_permute(mz[d], "col", d) for d in range(1, 4)]
    scratch = [(4, 2, 5, 8, E), (2, 2, 9, 16, E)]
    m = call(
        partial(join_kernel, ks), [pos, alog4] + r + c,
        [((5, 8, E), F32)] * 3 + [((9, 16, E), F32)] * 3,
        scratch + [(2, 5, 8, E), (2, 9, 16, E)], "join",
    )
    ym = [xor_permute(m[2 + d], "row", 2 * d) for d in range(1, 4)]
    xm = [xor_permute(m[d - 1], "col", 4 * d) for d in range(1, 4)]
    s = call(
        partial(start_kernel, ks), [pos, alog4] + r + c + xm + ym,
        [((2, 4, 8, E), F32)] * 4 + [((2, 8, 16, E), F32)] * 2,
        scratch + [(4, 5, 8, E), (4, 9, 16, E), (4, 2, 4, 8, E), (2, 2, 8, 16, E)], "starts",
    )
    t = [s[0]] + [xor_permute(s[d], "col", d) for d in range(1, 4)]
    u = [s[4], xor_permute(s[5], "row", 1)]
    return t + u


def passed_along(block, axis, distance):
    devices = range(lax.axis_size(axis))
    route = [(i - distance, i) for i in devices if i - distance in devices]
    return lax.ppermute(block, axis, route)


def per_device(
    image, in_weight, conv_weight, conv_bias, proj_weight, dt_weight, dt_bias, a_log,
    skip_gain, norm_gain, out_weight, cotangent,
):
    r, c = lax.axis_index("row"), lax.axis_index("col")
    pos = jnp.stack([c % 4, c // 4, r // 2, r % 2]).astype(jnp.int32)
    wide = image.astype(F32)
    up = passed_along(wide[H - 1 :], "row", 1)
    down = passed_along(wide[:1], "row", -1)
    tall = jnp.concatenate([up, wide, down], axis=0)
    left = passed_along(tall[:, W - 1 :], "col", 1)
    right = passed_along(tall[:, :1], "col", -1)
    pix = jnp.concatenate([left, tall, right, jnp.zeros((H + 2, 6, C), F32)], axis=1)
    img = image.reshape(H * W, C)
    cot = cotangent.reshape(H * W, C)
    cw = conv_weight.reshape(9, 1, E)
    cb = conv_bias.reshape(1, E)
    tail = jnp.zeros((E, 48), F32)
    p01w = jnp.concatenate([proj_weight[0], proj_weight[1], tail], axis=1)
    p23w = jnp.concatenate([proj_weight[2], proj_weight[3], tail], axis=1)
    dtw = jnp.stack(
        [jnp.pad(dt_weight[k], ((40 * (k % 2), 120 - 40 * (k % 2)), (0, 0))) for k in range(4)]
    )
    dtb = dt_bias.reshape(4, 1, E)
    alog = a_log.reshape(4 * N, E)
    alog4 = a_log.reshape(4, N, 1, E)
    gain = norm_gain.reshape(1, E)

    tok = ((H * W, E), F32)
    prj = ((H * W, 128), F32)
    msgs = [((2, 5, 8, E), F32)] * 4 + [((2, 9, 16, E), F32)] * 2
    rate = (4 * N, 8, E)
    four = (4, H * W, E)
    col, row = (2, N, 8, E), (2, N, 16, E)
    sums = [(2, 8, E), (2, 16, E)]
    hid_rc, hid_cr, conv, gate, z, p01, p23, *m = call(
        first_kernel,
        [pos, pix, img, in_weight, cw, cb, p01w, p23w, dtw, dtb, alog],
        [tok, tok, tok, tok, (four, F32), prj, prj] + msgs,
        [rate, four, (10, 24, E), col, sums[0], row, sums[1]],
        "first",
    )
    starts = exchange(pos, alog4, m[:4], m[4:], (0, 1, 2, 3))
    out, g_out, g_gate, gate_pix, dtot_rc, dtot_cr, *m = call(
        middle_kernel,
        [pos] + starts + [hid_rc, hid_cr, gate, z, p01, p23, alog, skip_gain, gain,
                          out_weight, in_weight, cot, img],
        [((H * W, C), BF16), ((E, C), F32), ((C, E), F32), ((H * W, C), F32), tok, tok] + msgs,
        [rate, four, tok[0], tok[0], col, row, sums[0], sums[1]],
        "middle",
    )
    ends = exchange(pos, alog4, m[:4], m[4:], (1, 0, 3, 2))
    msg, center = call(
        last_kernel,
        [pos] + starts + ends + [hid_rc, hid_cr, conv, z, p01, p23, dtot_rc, dtot_cr, alog,
                                 skip_gain, p01w, p23w, dtw, cw, in_weight, pix, g_out,
                                 g_gate, gate_pix],
        [((1024, 128), F32), ((H * W, C), F32)],
        [rate, four, col, row, col, row, (W + 1, N, 8, E), rate, tok[0], tok[0], prj[0], prj[0],
         four, (12, 32, E), (10, 24, C), (128, 128)],
        "last",
    )
    got = lax.all_to_all(msg.reshape(128, 8, 128), AXES, 0, 0, tiled=True)
    (back,) = call(sum_kernel, [got.reshape(1024, 128)], [((1024, 128), F32)], [], "sum")
    got = lax.all_to_all(back.reshape(128, 8, 128), AXES, 0, 0, tiled=True)
    g_pix, g_in, g_outw, g_a = call(
        finish_kernel, [got.reshape(1024, 128), center],
        [((H * W, C), BF16), ((C, 2 * E), F32), ((E, C), F32), ((4 * N, E), F32)],
        [(H, W, C)], "finish",
    )
    return (
        out.reshape(H, W, C), g_pix.reshape(H, W, C), g_in, g_outw, g_a.reshape(4, N, E),
    )


def solution(mesh):
    tile = P("row", "col", None)
    return jax.shard_map(
        per_device,
        mesh=mesh,
        in_specs=(tile,) + (P(),) * 10 + (tile,),
        out_specs=(tile, tile, P(), P(), P()),
        check_vma=False,
    )
```

```python
from functools import partial

import jax
import jax.numpy as jnp
from jax import lax
from jax.experimental import pallas as pl
from jax.experimental.pallas import tpu as pltpu
from jax.sharding import PartitionSpec as P

F32 = jnp.float32
BF16 = jnp.bfloat16
H, W, C, E, N = 8, 16, 128, 256, 16
LOG2E = 1.4426950408889634
LN2 = 0.6931471805599453
AXES = ("row", "col")


def split2(a):
    hi = a.astype(BF16)
    return hi, (a - hi.astype(F32)).astype(BF16)


def dot(a, b, dims):
    return lax.dot_general(a, b, (dims, ((), ())), preferred_element_type=F32)


NN = ((1,), (0,))
NT = ((1,), (1,))


def mm3(a, b, dims=NN):
    ah, al = split2(a)
    bh, bl = split2(b)
    return dot(ah, bh, dims) + (dot(ah, bl, dims) + dot(al, bh, dims))


def mm2(a, b, dims=NN):
    ah, al = split2(a)
    return dot(ah, b, dims) + dot(al, b, dims)


def mm2r(a, b, dims=NN):
    bh, bl = split2(b)
    return dot(a, bh, dims) + dot(a, bl, dims)


def permute_tokens(x, to_cr):
    o = lax.broadcasted_iota(jnp.int32, (128, 128), 0)
    i = lax.broadcasted_iota(jnp.int32, (128, 128), 1)
    if to_cr:
        hit = i == ((o & 7) * 16 + (o >> 3))
    else:
        hit = i == ((o & 15) * 8 + (o >> 4))
    m = jnp.where(hit, 1.0, 0.0).astype(BF16)
    hi = x.astype(BF16)
    rest = x - hi.astype(F32)
    mid = rest.astype(BF16)
    low = (rest - mid.astype(F32)).astype(BF16)
    return dot(m, hi, NN) + (dot(m, mid, NN) + dot(m, low, NN))


def softplus(z):
    return jnp.maximum(z, 0.0) + jnp.log1p(jnp.exp(-jnp.abs(z)))


def sigmoid(v):
    return 1.0 / (1.0 + jnp.exp(-v))


def spread(p, sel, dst):
    hi, lo = split2(p)
    dst[...] = dot(jnp.concatenate([hi, lo], axis=1), sel[...], NN)


def lanes(ref, k, at, n):
    v = ref[k, at, 128 * n : 128 * n + 128]
    return jnp.concatenate([v, v], axis=1)


def fold(v):
    return v[:, :128] + v[:, 128:]


def fill_rates(alog, rate):
    r = -jnp.exp(alog[...]) * LOG2E
    for i in range(4 * N):
        rate[i] = jnp.broadcast_to(r[i : i + 1], (8, E))


def steps(k):
    return W if k < 2 else H


def groups(k):
    return (0,) if k < 2 else (0, 1)


def row_at(k, g, i):
    t = i if k % 2 == 0 else steps(k) - 1 - i
    start = t * 8 if k < 2 else t * 16 + g * 8
    return pl.multiple_of(start, 8)


def send_layout(pos, col_f, col_d, row_f, row_d, mz, mc):
    z, core = pos[0], pos[3]
    for d in range(4):
        q = jnp.bitwise_xor(z, d)
        for f in range(2):
            mz[d][f, 0:4] = col_f[f, pl.ds(4 * q, 4)]
            mz[d][f, 4] = col_d[f]
    for d in range(2):
        h = jnp.bitwise_xor(core, d)
        for f in range(2):
            mc[d][f, 0:8] = row_f[f, pl.ds(8 * h, 8)]
            mc[d][f, 8] = row_d[f]


def first_kernel(
    pos, pix, img, win, cw, cb, pw, dtw, dtb, alog, sel,
    hid_rc, hid_cr, conv, gate, z, proj, mz0, mz1, mz2, mz3, mc0, mc1,
    rate, delta, mix, col_f, col_d, row_f, row_d, bb,
):
    fill_rates(alog, rate)
    x = pix[...].reshape(10 * 24, C).astype(BF16)
    mix[...] = dot(x, win[:, :E], NN).reshape(10, 24, E)
    gate[...] = dot(img[...], win[:, E:], NN)
    acc = jnp.broadcast_to(cb[...].reshape(1, 1, E), (H, W, E))
    for j in range(3):
        for i in range(3):
            acc = acc + mix[i : i + H, j : j + W, :] * cw[3 * i + j].reshape(1, 1, E)
    acc = acc.reshape(H * W, E)
    conv[...] = acc
    hid = acc * sigmoid(acc)
    hid_rc[...] = hid
    cr = permute_tokens(hid, True)
    hid_cr[...] = cr
    for k in range(4):
        pk = mm3(cr if k < 2 else hid, pw[k])
        proj[k] = pk
        spread(pk, sel, bb.at[k])
        zk = mm3(pk, dtw[k]) + dtb[k]
        z[k] = zk
        delta[k] = softplus(zk)
    for k in range(4):
        h = hid_cr if k < 2 else hid_rc
        for g in groups(k):

            def body(i, s, k=k, g=g, h=h):
                at = pl.ds(row_at(k, g, i), 8)
                d = delta[k, at, :]
                u = d * h[at, :]
                new = [
                    jnp.exp2(d * rate[k * N + n]) * s[n] + u * lanes(bb, k, at, n)
                    for n in range(N)
                ]
                return tuple(new) + (s[N] + d,)

            zero = jnp.zeros((8, E), F32)
            s = lax.fori_loop(0, steps(k), body, (zero,) * (N + 1))
            f = k % 2
            if k < 2:
                for n in range(N):
                    col_f[f, n] = s[n]
                col_d[f] = s[N]
            else:
                for n in range(N):
                    row_f[f, n, 8 * g : 8 * g + 8, :] = s[n]
                row_d[f, 8 * g : 8 * g + 8, :] = s[N]
    send_layout(pos, col_f, col_d, row_f, row_d, (mz0, mz1, mz2, mz3), (mc0, mc1))


def decay(alog, k, n, d):
    r = -jnp.exp(alog[k, n]) * LOG2E
    return jnp.exp2(d * jnp.broadcast_to(r, d.shape))


def join_kernel(ks, pos, alog, r0, r1, r2, r3, c0, c1, mx1, mx2, mx3, my1, my2, my3, rs, rc, gx, gy):
    z, x, y, core = pos[0], pos[1], pos[2], pos[3]
    for d, r in enumerate((r0, r1, r2, r3)):
        rs[jnp.bitwise_xor(z, d)] = r[...]
    for d, r in enumerate((c0, c1)):
        rc[jnp.bitwise_xor(core, d)] = r[...]
    for f in range(2):
        order = range(4) if f == 0 else range(3, -1, -1)
        for n in range(4):
            total = None
            for t in order:
                piece = rs[t, f, n]
                total = piece if total is None else (
                    total * decay(alog, ks[f], 4 * z + n, rs[t, f, 4]) + piece
                )
            gx[f, n] = total
        gx[f, 4] = rs[0, f, 4] + rs[1, f, 4] + rs[2, f, 4] + rs[3, f, 4]
        one, two = (0, 1) if f == 0 else (1, 0)
        for n in range(8):
            gy[f, n] = (
                rc[one, f, n] * decay(alog, ks[2 + f], 8 * core + n, rc[two, f, 8])
                + rc[two, f, n]
            )
        gy[f, 8] = rc[0, f, 8] + rc[1, f, 8]
    for d, m in ((1, mx1), (2, mx2), (3, mx3)):
        m[...] = gx[jnp.where(jnp.bitwise_xor(x, d) > x, 0, 1)]
    for d, m in ((1, my1), (2, my2), (3, my3)):
        m[...] = gy[jnp.where(jnp.bitwise_xor(y, d) > y, 0, 1)]


def start_kernel(
    ks, pos, alog, r0, r1, r2, r3, c0, c1, x1, x2, x3, y1, y2, y3,
    so0, so1, so2, so3, co0, co1, rs, rc, xs, ys, oz, oc,
):
    z, x, y, core = pos[0], pos[1], pos[2], pos[3]
    for d, r in enumerate((r0, r1, r2, r3)):
        rs[jnp.bitwise_xor(z, d)] = r[...]
    for d, r in enumerate((c0, c1)):
        rc[jnp.bitwise_xor(core, d)] = r[...]
    xs[x] = jnp.zeros((5, 8, E), F32)
    ys[y] = jnp.zeros((9, 16, E), F32)
    for d, r in ((1, x1), (2, x2), (3, x3)):
        xs[jnp.bitwise_xor(x, d)] = r[...]
    for d, r in ((1, y1), (2, y2), (3, y3)):
        ys[jnp.bitwise_xor(y, d)] = r[...]
    for f in range(2):
        order = list(range(4)) if f == 0 else list(range(3, -1, -1))
        for n in range(4):
            s = jnp.zeros((8, E), F32)
            for p in order:
                before = p < x if f == 0 else p > x
                new = s * decay(alog, ks[f], 4 * z + n, xs[p, 4]) + xs[p, n]
                s = jnp.where(before, new, s)
            for t in order:
                oz[t, f, n] = s
                if t != order[-1]:
                    s = s * decay(alog, ks[f], 4 * z + n, rs[t, f, 4]) + rs[t, f, n]
        one, two = (0, 1) if f == 0 else (1, 0)
        for n in range(8):
            s = jnp.zeros((16, E), F32)
            for p in order:
                before = p < y if f == 0 else p > y
                new = s * decay(alog, ks[2 + f], 8 * core + n, ys[p, 8]) + ys[p, n]
                s = jnp.where(before, new, s)
            oc[one, f, n] = s
            oc[two, f, n] = (
                s * decay(alog, ks[2 + f], 8 * core + n, rc[one, f, 8]) + rc[one, f, n]
            )
    for d, o in enumerate((so0, so1, so2, so3)):
        o[...] = oz[jnp.bitwise_xor(z, d)]
    for d, o in enumerate((co0, co1)):
        o[...] = oc[jnp.bitwise_xor(core, d)]


def place_starts(pos, t, u, col_s, row_s):
    z, core = pos[0], pos[3]
    for d in range(4):
        q = jnp.bitwise_xor(z, d)
        for f in range(2):
            col_s[f, pl.ds(4 * q, 4)] = t[d][f]
    for d in range(2):
        h = jnp.bitwise_xor(core, d)
        for f in range(2):
            row_s[f, pl.ds(8 * h, 8)] = u[d][f]


def start_of(k, g, n, col_s, row_s, flip):
    f = (k % 2) ^ flip
    return col_s[f, n] if k < 2 else row_s[f, n, 8 * g : 8 * g + 8, :]


def middle_kernel(
    pos, t0, t1, t2, t3, u0, u1, hid_rc, hid_cr, gate, z, proj, alog, skip, gain,
    ow, win, cot, img, sel,
    out, g_out, g_gate, gate_pix, dtot_rc, dtot_cr, mz0, mz1, mz2, mz3, mc0, mc1,
    rate, delta, y01, y23, col_s, row_s, col_d, row_d, bb, cc,
):
    fill_rates(alog, rate)
    place_starts(pos, (t0, t1, t2, t3), (u0, u1), col_s, row_s)
    for k in range(4):
        delta[k] = softplus(z[k])
        spread(proj[k], sel, bb.at[k])
        spread(pltpu.roll(proj[k], 128 - N, 1), sel, cc.at[k])
    for k in range(4):
        h, yy = (hid_cr, y01) if k < 2 else (hid_rc, y23)
        for g in groups(k):

            def body(i, s, k=k, g=g, h=h, yy=yy):
                at = pl.ds(row_at(k, g, i), 8)
                d = delta[k, at, :]
                u = d * h[at, :]
                y = None
                new = []
                for n in range(N):
                    v = jnp.exp2(d * rate[k * N + n]) * s[n] + u * lanes(bb, k, at, n)
                    new.append(v)
                    c = v * lanes(cc, k, at, n)
                    y = c if y is None else y + c
                yy[at, :] = y if k % 2 == 0 else yy[at, :] + y
                return tuple(new)

            s = tuple(start_of(k, g, n, col_s, row_s, 0) for n in range(N))
            lax.fori_loop(0, steps(k), body, s)
    skips = skip[0:1] + skip[1:2] + skip[2:3] + skip[3:4]
    total = y23[...] + permute_tokens(y01[...], False) + skips * hid_rc[...]
    centered = total - jnp.mean(total, axis=-1, keepdims=True)
    inv = lax.rsqrt(jnp.mean(centered * centered, axis=-1, keepdims=True) + 1e-05)
    unit = centered * inv
    normed = unit * gain[...]
    gv = gate[...]
    sg = sigmoid(gv)
    act = gv * sg
    gated = normed * act
    out[...] = mm2(gated, ow[...]).astype(BF16)
    g_out[...] = mm2(gated.T, cot[...])
    dgated = dot(cot[...], ow[...], NT)
    dgate = dgated * normed * (sg * (1.0 + gv * (1.0 - sg)))
    imt = img[...].astype(F32).T.astype(BF16)
    g_gate[...] = mm2r(imt, dgate)
    gate_pix[...] = mm2(dgate, win[:, E:], NT)
    dn = dgated * act * gain[...]
    dt = inv * (
        dn
        - jnp.mean(dn, axis=-1, keepdims=True)
        - unit * jnp.mean(dn * unit, axis=-1, keepdims=True)
    )
    dtot_rc[...] = dt
    dtot_cr[...] = permute_tokens(dt, True)
    for k in range(4):
        dy = dtot_cr if k < 2 else dtot_rc
        f = 1 - k % 2
        for g in groups(k):

            def back(i, s, k=k, g=g, dy=dy):
                at = pl.ds(row_at(k, g, steps(k) - 1 - i), 8)
                d = delta[k, at, :]
                t = dy[at, :]
                new = [
                    jnp.exp2(d * rate[k * N + n]) * (s[n] + t * lanes(cc, k, at, n))
                    for n in range(N)
                ]
                return tuple(new) + (s[N] + d,)

            zero = jnp.zeros((8, E), F32)
            s = lax.fori_loop(0, steps(k), back, (zero,) * (N + 1))
            if k < 2:
                for n in range(N):
                    col_s[f, n] = s[n]
                col_d[f] = s[N]
            else:
                for n in range(N):
                    row_s[f, n, 8 * g : 8 * g + 8, :] = s[n]
                row_d[f, 8 * g : 8 * g + 8, :] = s[N]
    send_layout(pos, col_s, col_d, row_s, row_d, (mz0, mz1, mz2, mz3), (mc0, mc1))


def last_kernel(
    pos, t0, t1, t2, t3, u0, u1, b0, b1, b2, b3, v0, v1,
    hid_rc, hid_cr, conv, z, proj, dtot_rc, dtot_cr, alog, skip,
    pw, dtw, cw, win, pix, g_out, g_gate, gate_pix, sel,
    msg, center,
    rate, delta, col_s, row_s, col_b, row_b, hist, drate, dx01, dx23, xb, xc, dz,
    zpad, gp, edge, bb, cc,
):
    fill_rates(alog, rate)
    place_starts(pos, (t0, t1, t2, t3), (u0, u1), col_s, row_s)
    place_starts(pos, (b0, b1, b2, b3), (v0, v1), col_b, row_b)
    for k in range(4):
        delta[k] = softplus(z[k])
        spread(proj[k], sel, bb.at[k])
        spread(pltpu.roll(proj[k], 128 - N, 1), sel, cc.at[k])
    drate[...] = jnp.zeros_like(drate)
    for k in range(4):
        h, dy, dx = (hid_cr, dtot_cr, dx01) if k < 2 else (hid_rc, dtot_rc, dx23)
        last = steps(k)
        for g in groups(k):

            def body(i, s, k=k, g=g, h=h):
                at = pl.ds(row_at(k, g, i), 8)
                d = delta[k, at, :]
                u = d * h[at, :]
                new = []
                for n in range(N):
                    hist[i, n] = s[n]
                    new.append(
                        jnp.exp2(d * rate[k * N + n]) * s[n] + u * lanes(bb, k, at, n)
                    )
                return tuple(new)

            s = tuple(start_of(k, g, n, col_s, row_s, 0) for n in range(N))
            s = lax.fori_loop(0, last, body, s)
            for n in range(N):
                hist[last, n] = s[n]

            def back(j, m, k=k, g=g, h=h, dy=dy, dx=dx, last=last):
                i = last - 1 - j
                at = pl.ds(row_at(k, g, i), 8)
                d = delta[k, at, :]
                xx = h[at, :]
                u = d * xx
                t = dy[at, :]
                du = jnp.zeros((8, E), F32)
                dd = jnp.zeros((8, E), F32)
                new = []
                for n in range(N):
                    r = rate[k * N + n]
                    lam = lanes(cc, k, at, n) * t + m[n]
                    out = jnp.exp2(d * r) * lam
                    new.append(out)
                    xc[k, at, 128 * n : 128 * n + 128] = fold(t * hist[i + 1, n])
                    xb[k, at, 128 * n : 128 * n + 128] = fold(lam * u)
                    du = du + lam * lanes(bb, k, at, n)
                    q = out * hist[i, n]
                    dd = dd + q * r
                    drate[k * N + n] = drate[k * N + n] + q * d
                ddel = du * xx + dd * LN2
                dz[k, at, :] = ddel * sigmoid(z[k, at, :])
                dxv = du * d + skip[k : k + 1] * t
                if k % 2 == 0:
                    dx[at, :] = dxv
                else:
                    dx[at, :] = dx[at, :] + dxv
                return tuple(new)

            m = tuple(start_of(k, g, n, col_b, row_b, 1) for n in range(N))
            lax.fori_loop(0, last, back, m)
    g_a = jnp.sum(drate[...], axis=1) * (-jnp.exp(alog[...]))
    dcr, drc = dx01[...], dx23[...]
    pick = sel[0:128, :]
    for k in range(4):
        dpk = (
            mm3(dz[k], dtw[k], NT)
            + mm2(xb[k], pick, NT)
            + pltpu.roll(mm2(xc[k], pick, NT), N, 1)
        )
        dhk = mm3(dpk, pw[k], NT)
        if k < 2:
            dcr = dcr + dhk
        else:
            drc = drc + dhk
    dhid = drc + permute_tokens(dcr, False)
    cv = conv[...]
    sg = sigmoid(cv)
    dconv = dhid * (sg * (1.0 + cv * (1.0 - sg)))
    zpad[...] = jnp.zeros_like(zpad)
    zpad[2:10, 8:24, :] = dconv.reshape(H, W, E)
    acc = jnp.zeros((10, 24, E), F32)
    for j in range(3):
        for i in range(3):
            acc = acc + zpad[2 - i : 12 - i, 8 - j : 32 - j, :] * cw[3 * i + j].reshape(1, 1, E)
    flat = acc.reshape(240, E)
    gp[...] = mm2(flat, win[:, :E], NT).reshape(10, 24, C)
    pt = pix[...].reshape(240, C)
    g_in = mm2r(pt.T.astype(BF16), flat)
    center[...] = gate_pix[...] + gp[1:9, 1:17, :].reshape(128, C)
    edge[...] = jnp.zeros_like(edge)
    edge[0:16] = gp[9, 1:17, :]
    edge[16:32] = gp[0, 1:17, :]
    edge[32:40] = gp[1:9, 17, :]
    edge[40:48] = gp[1:9, 0, :]
    edge[48:49] = gp[9, 17:18, :]
    edge[49:50] = gp[9, 0:1, :]
    edge[50:51] = gp[0, 17:18, :]
    edge[51:52] = gp[0, 0:1, :]
    blocks = (
        g_in[:, :128],
        g_in[:, 128:],
        g_gate[:, :128],
        g_gate[:, 128:],
        g_out[:128],
        g_out[128:],
        jnp.concatenate([g_a[:, :128], g_a[:, 128:]], axis=0),
        edge[...].T,
    )
    for b, block in enumerate(blocks):
        msg[pl.ds(b, 128, stride=8), :] = block


def sum_kernel(r, o):
    s = jnp.sum(r[...].reshape(128, 8, 128), axis=0)
    h = r[pl.ds(7, 128, stride=8), :]
    d = lax.broadcasted_iota(jnp.int32, (128, 128), 0)
    i = lax.broadcasted_iota(jnp.int32, (128, 128), 1)
    rr, cc = d >> 4, d & 15
    inn = jnp.zeros((128, 128), F32)
    for lo, hi, dr, dc in (
        (0, 16, -1, 0), (16, 32, 1, 0), (32, 40, 0, -1), (40, 48, 0, 1),
        (48, 49, -1, -1), (49, 50, -1, 1), (50, 51, 1, -1), (51, 52, 1, 1),
    ):
        moved = pltpu.roll(h, (-(dr * 16 + dc)) % 128, 0)
        ok = (i >= lo) & (i < hi)
        ok = ok & (rr + dr >= 0) & (rr + dr < 8) & (cc + dc >= 0) & (cc + dc < 16)
        inn = jnp.where(ok, moved, inn)
    o[...] = jnp.broadcast_to(s[None], (128, 8, 128)).reshape(1024, 128)
    o[pl.ds(7, 128, stride=8), :] = inn


def finish_kernel(q, center, g_pix, g_in, g_out, g_a, acc):
    def block(b):
        return q[pl.ds(b, 128, stride=8), :]

    for b in range(4):
        g_in[:, 128 * b : 128 * b + 128] = block(b)
    g_out[:128] = block(4)
    g_out[128:] = block(5)
    a = block(6)
    g_a[:, :128] = a[:64]
    g_a[:, 128:] = a[64:]
    inn = block(7).T
    acc[...] = center[...].reshape(H, W, C)
    acc[0] = acc[0] + inn[0:16]
    acc[7] = acc[7] + inn[16:32]
    acc[:, 0, :] = acc[:, 0, :] + inn[32:40]
    acc[:, 15, :] = acc[:, 15, :] + inn[40:48]
    acc[0, 0:1, :] = acc[0, 0:1, :] + inn[48:49]
    acc[0, 15:16, :] = acc[0, 15:16, :] + inn[49:50]
    acc[7, 0:1, :] = acc[7, 0:1, :] + inn[50:51]
    acc[7, 15:16, :] = acc[7, 15:16, :] + inn[51:52]
    g_pix[...] = acc[...].reshape(H * W, C).astype(BF16)


def call(kernel, ins, outs, scratch, name):
    vmem = pl.BlockSpec(memory_space=pltpu.VMEM)
    specs = [
        pl.BlockSpec(memory_space=pltpu.SMEM) if x.dtype == jnp.int32 else vmem for x in ins
    ]
    return pl.pallas_call(
        kernel,
        out_shape=[jax.ShapeDtypeStruct(s, t) for s, t in outs],
        in_specs=specs,
        out_specs=[vmem] * len(outs),
        scratch_shapes=[pltpu.VMEM(s, F32) for s in scratch],
        compiler_params=pltpu.CompilerParams(vmem_limit_bytes=44 * 1024 * 1024),
        name=name,
    )(*ins)


def xor_permute(x, axis, mask):
    return lax.ppermute(x, axis, [(i, i ^ mask) for i in range(lax.axis_size(axis))])


def exchange(pos, alog4, mz, mc, ks):
    c = [mc[0], xor_permute(mc[1], "row", 1)]
    r = [mz[0]] + [xor_permute(mz[d], "col", d) for d in range(1, 4)]
    scratch = [(4, 2, 5, 8, E), (2, 2, 9, 16, E)]
    m = call(
        partial(join_kernel, ks), [pos, alog4] + r + c,
        [((5, 8, E), F32)] * 3 + [((9, 16, E), F32)] * 3,
        scratch + [(2, 5, 8, E), (2, 9, 16, E)], "join",
    )
    ym = [xor_permute(m[2 + d], "row", 2 * d) for d in range(1, 4)]
    xm = [xor_permute(m[d - 1], "col", 4 * d) for d in range(1, 4)]
    s = call(
        partial(start_kernel, ks), [pos, alog4] + r + c + xm + ym,
        [((2, 4, 8, E), F32)] * 4 + [((2, 8, 16, E), F32)] * 2,
        scratch + [(4, 5, 8, E), (4, 9, 16, E), (4, 2, 4, 8, E), (2, 2, 8, 16, E)], "starts",
    )
    t = [s[0]] + [xor_permute(s[d], "col", d) for d in range(1, 4)]
    u = [s[4], xor_permute(s[5], "row", 1)]
    return t + u


def passed_along(block, axis, distance):
    devices = range(lax.axis_size(axis))
    route = [(i - distance, i) for i in devices if i - distance in devices]
    return lax.ppermute(block, axis, route)


def per_device(
    image, in_weight, conv_weight, conv_bias, proj_weight, dt_weight, dt_bias, a_log,
    skip_gain, norm_gain, out_weight, cotangent,
):
    r, c = lax.axis_index("row"), lax.axis_index("col")
    pos = jnp.stack([c % 4, c // 4, r // 2, r % 2]).astype(jnp.int32)
    wide = image.astype(F32)
    up = passed_along(wide[H - 1 :], "row", 1)
    down = passed_along(wide[:1], "row", -1)
    tall = jnp.concatenate([up, wide, down], axis=0)
    left = passed_along(tall[:, W - 1 :], "col", 1)
    right = passed_along(tall[:, :1], "col", -1)
    pix = jnp.concatenate([left, tall, right, jnp.zeros((H + 2, 6, C), F32)], axis=1)
    img = image.reshape(H * W, C)
    cot = cotangent.reshape(H * W, C)
    cw = conv_weight.reshape(9, 1, E)
    cb = conv_bias.reshape(1, E)
    pw = jnp.pad(proj_weight, ((0, 0), (0, 0), (0, 88)))
    dtw = jnp.pad(dt_weight, ((0, 0), (0, 120), (0, 0)))
    entry = lax.broadcasted_iota(jnp.int32, (256, N * 128), 0) & 127
    state = lax.broadcasted_iota(jnp.int32, (256, N * 128), 1) >> 7
    sel = jnp.where(entry == state + 8, 1.0, 0.0).astype(BF16)
    dtb = dt_bias.reshape(4, 1, E)
    alog = a_log.reshape(4 * N, E)
    alog4 = a_log.reshape(4, N, 1, E)
    gain = norm_gain.reshape(1, E)

    tok = ((H * W, E), F32)
    prj = ((4, H * W, 128), F32)
    wide_rows = (4, H * W, N * 128)
    msgs = [((2, 5, 8, E), F32)] * 4 + [((2, 9, 16, E), F32)] * 2
    rate = (4 * N, 8, E)
    four = (4, H * W, E)
    col, row = (2, N, 8, E), (2, N, 16, E)
    sums = [(2, 8, E), (2, 16, E)]
    hid_rc, hid_cr, conv, gate, z, proj, *m = call(
        first_kernel,
        [pos, pix, img, in_weight, cw, cb, pw, dtw, dtb, alog, sel],
        [tok, tok, tok, tok, (four, F32), prj] + msgs,
        [rate, four, (10, 24, E), col, sums[0], row, sums[1], wide_rows],
        "first",
    )
    starts = exchange(pos, alog4, m[:4], m[4:], (0, 1, 2, 3))
    out, g_out, g_gate, gate_pix, dtot_rc, dtot_cr, *m = call(
        middle_kernel,
        [pos] + starts + [hid_rc, hid_cr, gate, z, proj, alog, skip_gain, gain,
                          out_weight, in_weight, cot, img, sel],
        [((H * W, C), BF16), ((E, C), F32), ((C, E), F32), ((H * W, C), F32), tok, tok] + msgs,
        [rate, four, tok[0], tok[0], col, row, sums[0], sums[1], wide_rows, wide_rows],
        "middle",
    )
    ends = exchange(pos, alog4, m[:4], m[4:], (1, 0, 3, 2))
    msg, center = call(
        last_kernel,
        [pos] + starts + ends + [hid_rc, hid_cr, conv, z, proj, dtot_rc, dtot_cr, alog,
                                 skip_gain, pw, dtw, cw, in_weight, pix, g_out,
                                 g_gate, gate_pix, sel],
        [((1024, 128), F32), ((H * W, C), F32)],
        [rate, four, col, row, col, row, (W + 1, N, 8, E), rate, tok[0], tok[0], wide_rows, wide_rows,
         four, (12, 32, E), (10, 24, C), (128, 128), wide_rows, wide_rows],
        "last",
    )
    got = lax.all_to_all(msg.reshape(128, 8, 128), AXES, 0, 0, tiled=True)
    (back,) = call(sum_kernel, [got.reshape(1024, 128)], [((1024, 128), F32)], [], "sum")
    got = lax.all_to_all(back.reshape(128, 8, 128), AXES, 0, 0, tiled=True)
    g_pix, g_in, g_outw, g_a = call(
        finish_kernel, [got.reshape(1024, 128), center],
        [((H * W, C), BF16), ((C, 2 * E), F32), ((E, C), F32), ((4 * N, E), F32)],
        [(H, W, C)], "finish",
    )
    return (
        out.reshape(H, W, C), g_pix.reshape(H, W, C), g_in, g_outw, g_a.reshape(4, N, E),
    )


def solution(mesh):
    tile = P("row", "col", None)
    return jax.shard_map(
        per_device,
        mesh=mesh,
        in_specs=(tile,) + (P(),) * 10 + (tile,),
        out_specs=(tile, tile, P(), P(), P()),
        check_vma=False,
    )
```

```python
from functools import partial

import jax
import jax.numpy as jnp
from jax import lax
from jax.experimental import pallas as pl
from jax.experimental.pallas import tpu as pltpu
from jax.sharding import PartitionSpec as P

F32 = jnp.float32
BF16 = jnp.bfloat16
H, W, C, E, N = 8, 16, 128, 256, 16
LOG2E = 1.4426950408889634
LN2 = 0.6931471805599453
AXES = ("row", "col")


def split2(a):
    hi = a.astype(BF16)
    return hi, (a - hi.astype(F32)).astype(BF16)


def dot(a, b, dims):
    return lax.dot_general(a, b, (dims, ((), ())), preferred_element_type=F32)


NN = ((1,), (0,))
NT = ((1,), (1,))


def mm3(a, b, dims=NN):
    ah, al = split2(a)
    bh, bl = split2(b)
    return dot(ah, bh, dims) + (dot(ah, bl, dims) + dot(al, bh, dims))


def mm2(a, b, dims=NN):
    ah, al = split2(a)
    return dot(ah, b, dims) + dot(al, b, dims)


def mm2r(a, b, dims=NN):
    bh, bl = split2(b)
    return dot(a, bh, dims) + dot(a, bl, dims)


def permute_tokens(x, to_cr):
    o = lax.broadcasted_iota(jnp.int32, (128, 128), 0)
    i = lax.broadcasted_iota(jnp.int32, (128, 128), 1)
    if to_cr:
        hit = i == ((o & 7) * 16 + (o >> 3))
    else:
        hit = i == ((o & 15) * 8 + (o >> 4))
    m = jnp.where(hit, 1.0, 0.0).astype(BF16)
    hi = x.astype(BF16)
    rest = x - hi.astype(F32)
    mid = rest.astype(BF16)
    low = (rest - mid.astype(F32)).astype(BF16)
    return dot(m, hi, NN) + (dot(m, mid, NN) + dot(m, low, NN))


def softplus(z):
    return jnp.maximum(z, 0.0) + jnp.log1p(jnp.exp(-jnp.abs(z)))


def sigmoid(v):
    return 1.0 / (1.0 + jnp.exp(-v))


def spread(p, sel, dst):
    hi, lo = split2(p)
    dst[...] = dot(jnp.concatenate([hi, lo], axis=1), sel[...], NN)


def lanes(ref, k, at, n):
    v = ref[k, at, 128 * n : 128 * n + 128]
    return jnp.concatenate([v, v], axis=1)


def fold(v):
    return v[:, :128] + v[:, 128:]


def fill_rates(alog, rate):
    r = -jnp.exp(alog[...]) * LOG2E
    for i in range(4 * N):
        rate[i] = jnp.broadcast_to(r[i : i + 1], (8, E))


def steps(k):
    return W if k < 2 else H


def groups(k):
    return (0,) if k < 2 else (0, 1)


def row_at(k, g, i):
    t = i if k % 2 == 0 else steps(k) - 1 - i
    start = t * 8 if k < 2 else t * 16 + g * 8
    return pl.multiple_of(start, 8)


def end_states(k, g, delta, h, rate, bb):
    def body(i, s):
        at = pl.ds(row_at(k, g, i), 8)
        d = delta[k, at, :]
        u = d * h[at, :]
        new = [
            jnp.exp2(d * rate[k * N + n]) * s[n] + u * lanes(bb, k % 2, at, n) for n in range(N)
        ]
        return tuple(new) + (s[N] + d,)

    return lax.fori_loop(0, steps(k), body, (jnp.zeros((8, E), F32),) * (N + 1))


def outputs(k, g, start, delta, h, rate, bb, cc, yy):
    def body(i, s):
        at = pl.ds(row_at(k, g, i), 8)
        d = delta[k, at, :]
        u = d * h[at, :]
        y = None
        new = []
        for n in range(N):
            v = jnp.exp2(d * rate[k * N + n]) * s[n] + u * lanes(bb, k % 2, at, n)
            new.append(v)
            c = v * lanes(cc, k % 2, at, n)
            y = c if y is None else y + c
        yy[at, :] = y if k % 2 == 0 else yy[at, :] + y
        return tuple(new)

    lax.fori_loop(0, steps(k), body, start)


def end_adjoints(k, g, delta, dy, rate, cc):
    def body(j, s):
        at = pl.ds(row_at(k, g, steps(k) - 1 - j), 8)
        d = delta[k, at, :]
        t = dy[at, :]
        new = [
            jnp.exp2(d * rate[k * N + n]) * (s[n] + t * lanes(cc, k % 2, at, n))
            for n in range(N)
        ]
        return tuple(new) + (s[N] + d,)

    return lax.fori_loop(0, steps(k), body, (jnp.zeros((8, E), F32),) * (N + 1))


def history(k, g, start, delta, h, rate, bb, hist):
    def body(i, s):
        at = pl.ds(row_at(k, g, i), 8)
        d = delta[k, at, :]
        u = d * h[at, :]
        new = []
        for n in range(N):
            hist[i, n] = s[n]
            new.append(jnp.exp2(d * rate[k * N + n]) * s[n] + u * lanes(bb, k % 2, at, n))
        return tuple(new)

    s = lax.fori_loop(0, steps(k), body, start)
    for n in range(N):
        hist[steps(k), n] = s[n]


def gradients(k, g, end, delta, sig, h, dy, rate, bb, cc, hist, skip, xb, xc, dz, dx, drate):
    kk = k % 2

    def body(j, m):
        i = steps(k) - 1 - j
        at = pl.ds(row_at(k, g, i), 8)
        d = delta[k, at, :]
        xx = h[at, :]
        u = d * xx
        t = dy[at, :]
        du = jnp.zeros((8, E), F32)
        dd = jnp.zeros((8, E), F32)
        new = []
        for n in range(N):
            r = rate[k * N + n]
            lam = lanes(cc, kk, at, n) * t + m[n]
            out = jnp.exp2(d * r) * lam
            new.append(out)
            xc[kk, at, 128 * n : 128 * n + 128] = fold(t * hist[i + 1, n])
            xb[kk, at, 128 * n : 128 * n + 128] = fold(lam * u)
            du = du + lam * lanes(bb, kk, at, n)
            q = out * hist[i, n]
            dd = dd + q * r
            drate[kk * N + n] = drate[kk * N + n] + q * d
        dz[kk, at, :] = (du * xx + dd * LN2) * sig[k, at, :]
        dxv = du * d + skip[k : k + 1] * t
        dx[at, :] = dxv if kk == 0 else dx[at, :] + dxv
        return tuple(new)

    lax.fori_loop(0, steps(k), body, end)


def close_pair(first, dx, dz, xb, xc, dtw, pw, sel):
    total = dx[...]
    pick = sel[0:128, :]
    for kk in range(2):
        dp = (
            mm3(dz[kk], dtw[first + kk], NT)
            + mm2(xb[kk], pick, NT)
            + pltpu.roll(mm2(xc[kk], pick, NT), N, 1)
        )
        total = total + mm3(dp, pw[first + kk], NT)
    return total


def rate_gradient(drate, alog, first):
    return jnp.sum(drate[...], axis=1) * (-jnp.exp(alog[N * first : N * first + 2 * N]))


def keep_col(f, s, col_f, col_d):
    for n in range(N):
        col_f[f, n] = s[n]
    col_d[f] = s[N]


def col_message(pos, col_f, col_d, mz):
    for d in range(4):
        q = jnp.bitwise_xor(pos[0], d)
        for f in range(2):
            mz[d][f, 0:4] = col_f[f, pl.ds(4 * q, 4)]
            mz[d][f, 4] = col_d[f]


def place_cols(pos, t, col_s):
    for d in range(4):
        q = jnp.bitwise_xor(pos[0], d)
        for f in range(2):
            col_s[f, pl.ds(4 * q, 4)] = t[d][f]


def col_start(col_s, f):
    return tuple(col_s[f, n] for n in range(N))


def keep_row(f, g, s, row_f, row_d):
    for n in range(N):
        row_f[f, n, 8 * g : 8 * g + 8, :] = s[n]
    row_d[f, 8 * g : 8 * g + 8, :] = s[N]


def row_message(pos, row_f, row_d, mc):
    for d in range(2):
        h = jnp.bitwise_xor(pos[3], d)
        for f in range(2):
            mc[d][f, 0:8] = row_f[f, pl.ds(8 * h, 8)]
            mc[d][f, 8] = row_d[f]


def place_rows(pos, u, row_s):
    for d in range(2):
        h = jnp.bitwise_xor(pos[3], d)
        for f in range(2):
            row_s[f, pl.ds(8 * h, 8)] = u[d][f]


def row_start(row_s, f, g):
    return tuple(row_s[f, n, 8 * g : 8 * g + 8, :] for n in range(N))


def first_kernel(
    pos, pix, img, win, cw, cb, pw, dtw, dtb, alog, sel,
    hid_rc, hid_cr, conv, gate, delta, sig, proj, rate, bb, mz0, mz1, mz2, mz3,
    mix, col_f, col_d,
):
    fill_rates(alog, rate)
    x = pix[...].reshape(10 * 24, C).astype(BF16)
    mix[...] = dot(x, win[:, :E], NN).reshape(10, 24, E)
    gate[...] = dot(img[...], win[:, E:], NN)
    acc = jnp.broadcast_to(cb[...].reshape(1, 1, E), (H, W, E))
    for j in range(3):
        for i in range(3):
            acc = acc + mix[i : i + H, j : j + W, :] * cw[3 * i + j].reshape(1, 1, E)
    acc = acc.reshape(H * W, E)
    conv[...] = acc
    hid = acc * sigmoid(acc)
    hid_rc[...] = hid
    cr = permute_tokens(hid, True)
    hid_cr[...] = cr
    for k in range(4):
        pk = mm3(cr if k < 2 else hid, pw[k])
        proj[k] = pk
        if k < 2:
            spread(pk, sel, bb.at[k])
        zk = mm3(pk, dtw[k]) + dtb[k]
        sig[k] = sigmoid(zk)
        delta[k] = softplus(zk)
    for k in range(2):
        keep_col(k, end_states(k, 0, delta, hid_cr, rate, bb), col_f, col_d)
    col_message(pos, col_f, col_d, (mz0, mz1, mz2, mz3))


def row_ends_kernel(pos, hid_rc, delta, proj, rate, sel, bb, mc0, mc1, row_f, row_d):
    for k in (2, 3):
        spread(proj[k], sel, bb.at[k - 2])
    for k in (2, 3):
        for g in (0, 1):
            keep_row(k - 2, g, end_states(k, g, delta, hid_rc, rate, bb), row_f, row_d)
    row_message(pos, row_f, row_d, (mc0, mc1))


def decay(alog, k, n, d):
    r = -jnp.exp(alog[k, n]) * LOG2E
    return jnp.exp2(d * jnp.broadcast_to(r, d.shape))


def join_kernel(ks, pos, alog, r0, r1, r2, r3, c0, c1, mx1, mx2, mx3, my1, my2, my3, rs, rc, gx, gy):
    z, x, y, core = pos[0], pos[1], pos[2], pos[3]
    for d, r in enumerate((r0, r1, r2, r3)):
        rs[jnp.bitwise_xor(z, d)] = r[...]
    for d, r in enumerate((c0, c1)):
        rc[jnp.bitwise_xor(core, d)] = r[...]
    for f in range(2):
        order = range(4) if f == 0 else range(3, -1, -1)
        for n in range(4):
            total = None
            for t in order:
                piece = rs[t, f, n]
                total = piece if total is None else (
                    total * decay(alog, ks[f], 4 * z + n, rs[t, f, 4]) + piece
                )
            gx[f, n] = total
        gx[f, 4] = rs[0, f, 4] + rs[1, f, 4] + rs[2, f, 4] + rs[3, f, 4]
        one, two = (0, 1) if f == 0 else (1, 0)
        for n in range(8):
            gy[f, n] = (
                rc[one, f, n] * decay(alog, ks[2 + f], 8 * core + n, rc[two, f, 8])
                + rc[two, f, n]
            )
        gy[f, 8] = rc[0, f, 8] + rc[1, f, 8]
    for d, m in ((1, mx1), (2, mx2), (3, mx3)):
        m[...] = gx[jnp.where(jnp.bitwise_xor(x, d) > x, 0, 1)]
    for d, m in ((1, my1), (2, my2), (3, my3)):
        m[...] = gy[jnp.where(jnp.bitwise_xor(y, d) > y, 0, 1)]


def start_kernel(
    ks, pos, alog, r0, r1, r2, r3, c0, c1, x1, x2, x3, y1, y2, y3,
    so0, so1, so2, so3, co0, co1, rs, rc, xs, ys, oz, oc,
):
    z, x, y, core = pos[0], pos[1], pos[2], pos[3]
    for d, r in enumerate((r0, r1, r2, r3)):
        rs[jnp.bitwise_xor(z, d)] = r[...]
    for d, r in enumerate((c0, c1)):
        rc[jnp.bitwise_xor(core, d)] = r[...]
    xs[x] = jnp.zeros((5, 8, E), F32)
    ys[y] = jnp.zeros((9, 16, E), F32)
    for d, r in ((1, x1), (2, x2), (3, x3)):
        xs[jnp.bitwise_xor(x, d)] = r[...]
    for d, r in ((1, y1), (2, y2), (3, y3)):
        ys[jnp.bitwise_xor(y, d)] = r[...]
    for f in range(2):
        order = list(range(4)) if f == 0 else list(range(3, -1, -1))
        for n in range(4):
            s = jnp.zeros((8, E), F32)
            for p in order:
                before = p < x if f == 0 else p > x
                new = s * decay(alog, ks[f], 4 * z + n, xs[p, 4]) + xs[p, n]
                s = jnp.where(before, new, s)
            for t in order:
                oz[t, f, n] = s
                if t != order[-1]:
                    s = s * decay(alog, ks[f], 4 * z + n, rs[t, f, 4]) + rs[t, f, n]
        one, two = (0, 1) if f == 0 else (1, 0)
        for n in range(8):
            s = jnp.zeros((16, E), F32)
            for p in order:
                before = p < y if f == 0 else p > y
                new = s * decay(alog, ks[2 + f], 8 * core + n, ys[p, 8]) + ys[p, n]
                s = jnp.where(before, new, s)
            oc[one, f, n] = s
            oc[two, f, n] = (
                s * decay(alog, ks[2 + f], 8 * core + n, rc[one, f, 8]) + rc[one, f, n]
            )
    for d, o in enumerate((so0, so1, so2, so3)):
        o[...] = oz[jnp.bitwise_xor(z, d)]
    for d, o in enumerate((co0, co1)):
        o[...] = oc[jnp.bitwise_xor(core, d)]


def row_out_kernel(
    pos, u0, u1, hid_rc, delta, proj, rate, bb, sel, yy, cc, row_s,
):
    place_rows(pos, (u0, u1), row_s)
    for k in (2, 3):
        spread(pltpu.roll(proj[k], 128 - N, 1), sel, cc.at[k - 2])
    for k in (2, 3):
        for g in (0, 1):
            outputs(k, g, row_start(row_s, k - 2, g), delta, hid_rc, rate, bb, cc, yy)


def middle_kernel(
    pos, t0, t1, t2, t3, hid_rc, hid_cr, gate, delta, proj, rate, bb, y23, skip, gain, ow,
    win, cot, img, sel,
    out, g_out, g_gate, gate_pix, dtot_rc, dtot_cr, cc, mz0, mz1, mz2, mz3,
    y01, col_s, col_d,
):
    place_cols(pos, (t0, t1, t2, t3), col_s)
    for k in range(2):
        spread(pltpu.roll(proj[k], 128 - N, 1), sel, cc.at[k])
    for k in range(2):
        outputs(k, 0, col_start(col_s, k), delta, hid_cr, rate, bb, cc, y01)
    skips = skip[0:1] + skip[1:2] + skip[2:3] + skip[3:4]
    total = y23[...] + permute_tokens(y01[...], False) + skips * hid_rc[...]
    centered = total - jnp.mean(total, axis=-1, keepdims=True)
    inv = lax.rsqrt(jnp.mean(centered * centered, axis=-1, keepdims=True) + 1e-05)
    unit = centered * inv
    normed = unit * gain[...]
    gv = gate[...]
    sg = sigmoid(gv)
    act = gv * sg
    gated = normed * act
    out[...] = mm2(gated, ow[...]).astype(BF16)
    g_out[...] = mm2(gated.T, cot[...])
    dgated = dot(cot[...], ow[...], NT)
    dgate = dgated * normed * (sg * (1.0 + gv * (1.0 - sg)))
    imt = img[...].astype(F32).T.astype(BF16)
    g_gate[...] = mm2r(imt, dgate)
    gate_pix[...] = mm2(dgate, win[:, E:], NT)
    dn = dgated * act * gain[...]
    dt = inv * (
        dn
        - jnp.mean(dn, axis=-1, keepdims=True)
        - unit * jnp.mean(dn * unit, axis=-1, keepdims=True)
    )
    dtot_rc[...] = dt
    dtot_cr[...] = permute_tokens(dt, True)
    for k in range(2):
        keep_col(1 - k, end_adjoints(k, 0, delta, dtot_cr, rate, cc), col_s, col_d)
    col_message(pos, col_s, col_d, (mz0, mz1, mz2, mz3))


def replay_kernel(pos, t0, t1, t2, t3, hid_cr, delta, rate, bb, hist, col_s):
    place_cols(pos, (t0, t1, t2, t3), col_s)
    for k in range(2):
        history(k, 0, col_start(col_s, k), delta, hid_cr, rate, bb, hist.at[k])


def row_replay_kernel(pos, u0, u1, hid_rc, delta, rate, bb, hist, row_s):
    place_rows(pos, (u0, u1), row_s)
    for k in (2, 3):
        for g in (0, 1):
            history(
                k, g, row_start(row_s, k - 2, g), delta, hid_rc, rate, bb,
                hist.at[2 * (k - 2) + g],
            )


def row_back_kernel(pos, delta, dtot_rc, rate, cc, mc0, mc1, row_f, row_d):
    for k in (2, 3):
        for g in (0, 1):
            keep_row(3 - k, g, end_adjoints(k, g, delta, dtot_rc, rate, cc), row_f, row_d)
    row_message(pos, row_f, row_d, (mc0, mc1))


def row_grad_kernel(
    pos, v0, v1, hist, hid_rc, delta, sig, rate, bb, cc, dtot_rc, skip, pw, dtw, alog, sel,
    drc, g_a,
    row_b, drate, dx, xb, xc, dz,
):
    place_rows(pos, (v0, v1), row_b)
    drate[...] = jnp.zeros_like(drate)
    for k in (2, 3):
        for g in (0, 1):
            gradients(
                k, g, row_start(row_b, 3 - k, g), delta, sig, hid_rc, dtot_rc, rate, bb, cc,
                hist.at[2 * (k - 2) + g], skip, xb, xc, dz, dx, drate,
            )
    g_a[...] = rate_gradient(drate, alog, 2)
    drc[...] = close_pair(2, dx, dz, xb, xc, dtw, pw, sel)


def last_kernel(
    pos, b0, b1, b2, b3, hist, hid_cr, conv, delta, sig, rate, bb, cc, dtot_cr, drc,
    g_a23, alog, skip, pw, dtw, cw, win, pix, g_out, g_gate, gate_pix, sel,
    msg, center,
    drate, dx, xb, xc, dz, col_b, zpad, gp, edge,
):
    place_cols(pos, (b0, b1, b2, b3), col_b)
    drate[...] = jnp.zeros_like(drate)
    for k in range(2):
        gradients(
            k, 0, col_start(col_b, 1 - k), delta, sig, hid_cr, dtot_cr, rate, bb, cc,
            hist.at[k], skip, xb, xc, dz, dx, drate,
        )
    g_a = jnp.concatenate([rate_gradient(drate, alog, 0), g_a23[...]], axis=0)
    dcr = close_pair(0, dx, dz, xb, xc, dtw, pw, sel)
    dhid = drc[...] + permute_tokens(dcr, False)
    cv = conv[...]
    sg = sigmoid(cv)
    dconv = dhid * (sg * (1.0 + cv * (1.0 - sg)))
    zpad[...] = jnp.zeros_like(zpad)
    zpad[2:10, 8:24, :] = dconv.reshape(H, W, E)
    acc = jnp.zeros((10, 24, E), F32)
    for j in range(3):
        for i in range(3):
            acc = acc + zpad[2 - i : 12 - i, 8 - j : 32 - j, :] * cw[3 * i + j].reshape(1, 1, E)
    flat = acc.reshape(240, E)
    gp[...] = mm2(flat, win[:, :E], NT).reshape(10, 24, C)
    pt = pix[...].reshape(240, C)
    g_in = mm2r(pt.T.astype(BF16), flat)
    center[...] = gate_pix[...] + gp[1:9, 1:17, :].reshape(128, C)
    edge[...] = jnp.zeros_like(edge)
    edge[0:16] = gp[9, 1:17, :]
    edge[16:32] = gp[0, 1:17, :]
    edge[32:40] = gp[1:9, 17, :]
    edge[40:48] = gp[1:9, 0, :]
    edge[48:49] = gp[9, 17:18, :]
    edge[49:50] = gp[9, 0:1, :]
    edge[50:51] = gp[0, 17:18, :]
    edge[51:52] = gp[0, 0:1, :]
    blocks = (
        g_in[:, :128],
        g_in[:, 128:],
        g_gate[:, :128],
        g_gate[:, 128:],
        g_out[:128],
        g_out[128:],
        jnp.concatenate([g_a[:, :128], g_a[:, 128:]], axis=0),
        edge[...].T,
    )
    for b, block in enumerate(blocks):
        msg[pl.ds(b, 128, stride=8), :] = block


def sum_kernel(r, o):
    s = jnp.sum(r[...].reshape(128, 8, 128), axis=0)
    h = r[pl.ds(7, 128, stride=8), :]
    d = lax.broadcasted_iota(jnp.int32, (128, 128), 0)
    i = lax.broadcasted_iota(jnp.int32, (128, 128), 1)
    rr, cc = d >> 4, d & 15
    inn = jnp.zeros((128, 128), F32)
    for lo, hi, dr, dc in (
        (0, 16, -1, 0), (16, 32, 1, 0), (32, 40, 0, -1), (40, 48, 0, 1),
        (48, 49, -1, -1), (49, 50, -1, 1), (50, 51, 1, -1), (51, 52, 1, 1),
    ):
        moved = pltpu.roll(h, (-(dr * 16 + dc)) % 128, 0)
        ok = (i >= lo) & (i < hi)
        ok = ok & (rr + dr >= 0) & (rr + dr < 8) & (cc + dc >= 0) & (cc + dc < 16)
        inn = jnp.where(ok, moved, inn)
    o[...] = jnp.broadcast_to(s[None], (128, 8, 128)).reshape(1024, 128)
    o[pl.ds(7, 128, stride=8), :] = inn


def finish_kernel(q, center, g_pix, g_in, g_out, g_a, acc):
    def block(b):
        return q[pl.ds(b, 128, stride=8), :]

    for b in range(4):
        g_in[:, 128 * b : 128 * b + 128] = block(b)
    g_out[:128] = block(4)
    g_out[128:] = block(5)
    a = block(6)
    g_a[:, :128] = a[:64]
    g_a[:, 128:] = a[64:]
    inn = block(7).T
    acc[...] = center[...].reshape(H, W, C)
    acc[0] = acc[0] + inn[0:16]
    acc[7] = acc[7] + inn[16:32]
    acc[:, 0, :] = acc[:, 0, :] + inn[32:40]
    acc[:, 15, :] = acc[:, 15, :] + inn[40:48]
    acc[0, 0:1, :] = acc[0, 0:1, :] + inn[48:49]
    acc[0, 15:16, :] = acc[0, 15:16, :] + inn[49:50]
    acc[7, 0:1, :] = acc[7, 0:1, :] + inn[50:51]
    acc[7, 15:16, :] = acc[7, 15:16, :] + inn[51:52]
    g_pix[...] = acc[...].reshape(H * W, C).astype(BF16)


def call(kernel, ins, outs, scratch, name, cost=1):
    vmem = pl.BlockSpec(memory_space=pltpu.VMEM)
    specs = [
        pl.BlockSpec(memory_space=pltpu.SMEM) if x.dtype == jnp.int32 else vmem for x in ins
    ]
    return pl.pallas_call(
        kernel,
        out_shape=[jax.ShapeDtypeStruct(s, t) for s, t in outs],
        in_specs=specs,
        out_specs=[vmem] * len(outs),
        scratch_shapes=[pltpu.VMEM(s, F32) for s in scratch],
        compiler_params=pltpu.CompilerParams(vmem_limit_bytes=14 * 1024 * 1024),
        cost_estimate=pl.CostEstimate(
            flops=0, bytes_accessed=cost * 3_500_000, transcendentals=0
        ),
        name=name,
    )(*ins)


def xor_permute(x, axis, mask):
    return lax.ppermute(x, axis, [(i, i ^ mask) for i in range(lax.axis_size(axis))])


def exchange(pos, alog4, mz, mc, ks):
    c = [mc[0], xor_permute(mc[1], "row", 1)]
    r = [mz[0]] + [xor_permute(mz[d], "col", d) for d in range(1, 4)]
    scratch = [(4, 2, 5, 8, E), (2, 2, 9, 16, E)]
    m = call(
        partial(join_kernel, ks), [pos, alog4] + r + c,
        [((5, 8, E), F32)] * 3 + [((9, 16, E), F32)] * 3,
        scratch + [(2, 5, 8, E), (2, 9, 16, E)], "join", 1,
    )
    ym = [xor_permute(m[2 + d], "row", 2 * d) for d in range(1, 4)]
    xm = [xor_permute(m[d - 1], "col", 4 * d) for d in range(1, 4)]
    s = call(
        partial(start_kernel, ks), [pos, alog4] + r + c + xm + ym,
        [((2, 4, 8, E), F32)] * 4 + [((2, 8, 16, E), F32)] * 2,
        scratch + [(4, 5, 8, E), (4, 9, 16, E), (4, 2, 4, 8, E), (2, 2, 8, 16, E)], "starts", 1,
    )
    t = [s[0]] + [xor_permute(s[d], "col", d) for d in range(1, 4)]
    u = [s[4], xor_permute(s[5], "row", 1)]
    return t, u


def rims(head, tail, axis):
    count = lax.axis_size(axis)
    mine = lax.axis_index(axis)
    odd = mine % 2 == 1
    near = xor_permute(jnp.where(odd, head, tail), axis, 1)
    pairs = [(i, (i + 1 if i % 2 == 1 else i - 1) % count) for i in range(count)]
    far = lax.ppermute(jnp.where(odd, tail, head), axis, pairs)
    before = jnp.where(mine == 0, 0.0, jnp.where(odd, near, far))
    after = jnp.where(mine == count - 1, 0.0, jnp.where(odd, far, near))
    return before, after


def per_device(
    image, in_weight, conv_weight, conv_bias, proj_weight, dt_weight, dt_bias, a_log,
    skip_gain, norm_gain, out_weight, cotangent,
):
    r, c = lax.axis_index("row"), lax.axis_index("col")
    pos = jnp.stack([c % 4, c // 4, r // 2, r % 2]).astype(jnp.int32)
    wide = image.astype(F32)
    up, down = rims(wide[:1], wide[H - 1 :], "row")
    tall = jnp.concatenate([up, wide, down], axis=0)
    left, right = rims(tall[:, :1], tall[:, W - 1 :], "col")
    pix = jnp.concatenate([left, tall, right, jnp.zeros((H + 2, 6, C), F32)], axis=1)
    img = image.reshape(H * W, C)
    cot = cotangent.reshape(H * W, C)
    cw = conv_weight.reshape(9, 1, E)
    cb = conv_bias.reshape(1, E)
    pw = jnp.pad(proj_weight, ((0, 0), (0, 0), (0, 88)))
    dtw = jnp.pad(dt_weight, ((0, 0), (0, 120), (0, 0)))
    entry = lax.broadcasted_iota(jnp.int32, (256, N * 128), 0) & 127
    state = lax.broadcasted_iota(jnp.int32, (256, N * 128), 1) >> 7
    sel = jnp.where(entry == state + 8, 1.0, 0.0).astype(BF16)
    dtb = dt_bias.reshape(4, 1, E)
    alog = a_log.reshape(4 * N, E)
    alog4 = a_log.reshape(4, N, 1, E)
    gain = norm_gain.reshape(1, E)

    tok = ((H * W, E), F32)
    four = (4, H * W, E)
    two = (2, H * W, E)
    rates = (4 * N, 8, E)
    prj = (4, H * W, 128)
    spreads = (2, H * W, N * 128)
    rows = [(2, N, 16, E), (2, 16, E)]
    cols = [(2, N, 8, E), (2, 8, E)]
    mcs = [((2, 9, 16, E), F32)] * 2
    mzs = [((2, 5, 8, E), F32)] * 4
    hid_rc, hid_cr, conv, gate, delta, sig, proj, rate, bb01, *mz = call(
        first_kernel,
        [pos, pix, img, in_weight, cw, cb, pw, dtw, dtb, alog, sel],
        [tok, tok, tok, tok, (four, F32), (four, F32), (prj, F32), (rates, F32),
         (spreads, F32)] + mzs,
        [(10, 24, E)] + cols, "first", 4,
    )
    bb23, *mc = call(
        row_ends_kernel, [pos, hid_rc, delta, proj, rate, sel], [(spreads, F32)] + mcs, rows,
        "row_ends", 3,
    )
    t, u = exchange(pos, alog4, mz, mc, (0, 1, 2, 3))
    y23, cc23 = call(
        row_out_kernel, [pos] + u + [hid_rc, delta, proj, rate, bb23, sel],
        [tok, (spreads, F32)], rows[:1], "row_out", 3,
    )
    out, g_out, g_gate, gate_pix, dtot_rc, dtot_cr, cc01, *mz = call(
        middle_kernel,
        [pos] + t + [hid_rc, hid_cr, gate, delta, proj, rate, bb01, y23, skip_gain, gain, out_weight,
                     in_weight, cot, img, sel],
        [((H * W, C), BF16), ((E, C), F32), ((C, E), F32), ((H * W, C), F32), tok, tok,
         (spreads, F32)] + mzs,
        [tok[0]] + cols, "middle", 5,
    )
    mc = call(
        row_back_kernel, [pos, delta, dtot_rc, rate, cc23], mcs, rows, "row_back", 3
    )
    (hist01,) = call(
        replay_kernel, [pos] + t + [hid_cr, delta, rate, bb01],
        [((2, W + 1, N, 8, E), F32)], cols[:1], "replay", 2,
    )
    (hist23,) = call(
        row_replay_kernel, [pos] + u + [hid_rc, delta, rate, bb23],
        [((4, H + 1, N, 8, E), F32)], rows[:1], "row_replay", 2,
    )
    b, v = exchange(pos, alog4, mz, mc, (1, 0, 3, 2))
    work = [(2 * N, 8, E), tok[0], spreads, spreads, two]
    drc, g_a23 = call(
        row_grad_kernel,
        [pos] + v + [hist23, hid_rc, delta, sig, rate, bb23, cc23, dtot_rc, skip_gain, pw, dtw,
                     alog, sel],
        [tok, ((2 * N, E), F32)],
        [rows[0]] + work, "row_grad", 7,
    )
    msg, center = call(
        last_kernel,
        [pos] + b + [hist01, hid_cr, conv, delta, sig, rate, bb01, cc01, dtot_cr, drc, g_a23,
                     alog, skip_gain, pw, dtw, cw, in_weight, pix, g_out, g_gate, gate_pix, sel],
        [((1024, 128), F32), ((H * W, C), F32)],
        work + [cols[0], (12, 32, E), (10, 24, C), (128, 128)],
        "last", 8,
    )
    got = lax.all_to_all(msg.reshape(128, 8, 128), AXES, 0, 0, tiled=True)
    (back,) = call(sum_kernel, [got.reshape(1024, 128)], [((1024, 128), F32)], [], "sum")
    got = lax.all_to_all(back.reshape(128, 8, 128), AXES, 0, 0, tiled=True)
    g_pix, g_in, g_outw, g_a = call(
        finish_kernel, [got.reshape(1024, 128), center],
        [((H * W, C), BF16), ((C, 2 * E), F32), ((E, C), F32), ((4 * N, E), F32)],
        [(H, W, C)], "finish",
    )
    return (
        out.reshape(H, W, C), g_pix.reshape(H, W, C), g_in, g_outw, g_a.reshape(4, N, E),
    )


def solution(mesh):
    tile = P("row", "col", None)
    return jax.shard_map(
        per_device,
        mesh=mesh,
        in_specs=(tile,) + (P(),) * 10 + (tile,),
        out_specs=(tile, tile, P(), P(), P()),
        check_vma=False,
    )
```

```python
from functools import partial

import jax
import jax.numpy as jnp
from jax import lax
from jax.experimental import pallas as pl
from jax.experimental.pallas import tpu as pltpu
from jax.sharding import PartitionSpec as P

F32 = jnp.float32
BF16 = jnp.bfloat16
H, W, C, E, N = 8, 16, 128, 256, 16
LOG2E = 1.4426950408889634
LN2 = 0.6931471805599453
AXES = ("row", "col")


def split2(a):
    hi = a.astype(BF16)
    return hi, (a - hi.astype(F32)).astype(BF16)


def dot(a, b, dims):
    return lax.dot_general(a, b, (dims, ((), ())), preferred_element_type=F32)


NN = ((1,), (0,))
NT = ((1,), (1,))


def mm3(a, b, dims=NN):
    ah, al = split2(a)
    bh, bl = split2(b)
    return dot(ah, bh, dims) + (dot(ah, bl, dims) + dot(al, bh, dims))


def mm2(a, b, dims=NN):
    ah, al = split2(a)
    return dot(ah, b, dims) + dot(al, b, dims)


def mm2r(a, b, dims=NN):
    bh, bl = split2(b)
    return dot(a, bh, dims) + dot(a, bl, dims)


def permute_tokens(x, to_cr):
    o = lax.broadcasted_iota(jnp.int32, (128, 128), 0)
    i = lax.broadcasted_iota(jnp.int32, (128, 128), 1)
    if to_cr:
        hit = i == ((o & 7) * 16 + (o >> 3))
    else:
        hit = i == ((o & 15) * 8 + (o >> 4))
    m = jnp.where(hit, 1.0, 0.0).astype(BF16)
    hi = x.astype(BF16)
    rest = x - hi.astype(F32)
    mid = rest.astype(BF16)
    low = (rest - mid.astype(F32)).astype(BF16)
    return dot(m, hi, NN) + (dot(m, mid, NN) + dot(m, low, NN))


def softplus(z):
    return jnp.maximum(z, 0.0) + jnp.log1p(jnp.exp(-jnp.abs(z)))


def sigmoid(v):
    return 1.0 / (1.0 + jnp.exp(-v))


def spread(p, sel, dst):
    hi, lo = split2(p)
    dst[...] = dot(jnp.concatenate([hi, lo], axis=1), sel[...], NN)


def lanes(ref, k, at, n):
    v = ref[k, at, 128 * n : 128 * n + 128]
    return jnp.concatenate([v, v], axis=1)


def fold(v):
    return v[:, :128] + v[:, 128:]


def fill_rates(alog, rate):
    r = -jnp.exp(alog[...]) * LOG2E
    for i in range(4 * N):
        rate[i] = jnp.broadcast_to(r[i : i + 1], (8, E))


def steps(k):
    return W if k < 2 else H


def groups(k):
    return (0,) if k < 2 else (0, 1)


def row_at(k, g, i):
    t = i if k % 2 == 0 else steps(k) - 1 - i
    start = t * 8 if k < 2 else t * 16 + g * 8
    return pl.multiple_of(start, 8)


def end_states(k, g, delta, h, rate, bb):
    def body(i, s):
        at = pl.ds(row_at(k, g, i), 8)
        d = delta[k, at, :]
        u = d * h[at, :]
        new = [
            jnp.exp2(d * rate[k * N + n]) * s[n] + u * lanes(bb, k % 2, at, n) for n in range(N)
        ]
        return tuple(new) + (s[N] + d,)

    return lax.fori_loop(0, steps(k), body, (jnp.zeros((8, E), F32),) * (N + 1))


def outputs(k, g, start, delta, h, rate, bb, cc, yy):
    def body(i, s):
        at = pl.ds(row_at(k, g, i), 8)
        d = delta[k, at, :]
        u = d * h[at, :]
        y = None
        new = []
        for n in range(N):
            v = jnp.exp2(d * rate[k * N + n]) * s[n] + u * lanes(bb, k % 2, at, n)
            new.append(v)
            c = v * lanes(cc, k % 2, at, n)
            y = c if y is None else y + c
        yy[at, :] = y if k % 2 == 0 else yy[at, :] + y
        return tuple(new)

    lax.fori_loop(0, steps(k), body, start)


def end_adjoints(k, g, delta, dy, rate, cc):
    def body(j, s):
        at = pl.ds(row_at(k, g, steps(k) - 1 - j), 8)
        d = delta[k, at, :]
        t = dy[at, :]
        new = [
            jnp.exp2(d * rate[k * N + n]) * (s[n] + t * lanes(cc, k % 2, at, n))
            for n in range(N)
        ]
        return tuple(new) + (s[N] + d,)

    return lax.fori_loop(0, steps(k), body, (jnp.zeros((8, E), F32),) * (N + 1))


def history(k, g, start, delta, h, rate, bb, hist):
    def body(i, s):
        at = pl.ds(row_at(k, g, i), 8)
        d = delta[k, at, :]
        u = d * h[at, :]
        new = []
        for n in range(N):
            hist[i, n] = s[n]
            new.append(jnp.exp2(d * rate[k * N + n]) * s[n] + u * lanes(bb, k % 2, at, n))
        return tuple(new)

    s = lax.fori_loop(0, steps(k), body, start)
    for n in range(N):
        hist[steps(k), n] = s[n]


def gradients(k, g, end, delta, sig, h, dy, rate, bb, cc, hist, skip, xb, xc, dz, dx, drate):
    kk = k % 2

    def body(j, m):
        i = steps(k) - 1 - j
        at = pl.ds(row_at(k, g, i), 8)
        d = delta[k, at, :]
        xx = h[at, :]
        u = d * xx
        t = dy[at, :]
        du = jnp.zeros((8, E), F32)
        dd = jnp.zeros((8, E), F32)
        new = []
        for n in range(N):
            r = rate[k * N + n]
            lam = lanes(cc, kk, at, n) * t + m[n]
            out = jnp.exp2(d * r) * lam
            new.append(out)
            xc[kk, at, 128 * n : 128 * n + 128] = fold(t * hist[i + 1, n])
            xb[kk, at, 128 * n : 128 * n + 128] = fold(lam * u)
            du = du + lam * lanes(bb, kk, at, n)
            q = out * hist[i, n]
            dd = dd + q * r
            drate[kk * N + n] = drate[kk * N + n] + q * d
        dz[kk, at, :] = (du * xx + dd * LN2) * sig[k, at, :]
        dxv = du * d + skip[k : k + 1] * t
        dx[at, :] = dxv if kk == 0 else dx[at, :] + dxv
        return tuple(new)

    lax.fori_loop(0, steps(k), body, end)


def close_pair(first, dx, dz, xb, xc, dtw, pw, sel):
    total = dx[...]
    pick = sel[0:128, :]
    for kk in range(2):
        dp = (
            mm3(dz[kk], dtw[first + kk], NT)
            + mm2(xb[kk], pick, NT)
            + pltpu.roll(mm2(xc[kk], pick, NT), N, 1)
        )
        total = total + mm3(dp, pw[first + kk], NT)
    return total


def rate_gradient(drate, alog, first):
    return jnp.sum(drate[...], axis=1) * (-jnp.exp(alog[N * first : N * first + 2 * N]))


def keep_col(f, s, col_f, col_d):
    for n in range(N):
        col_f[f, n] = s[n]
    col_d[f] = s[N]


def col_message(pos, col_f, col_d, mz):
    for d in range(4):
        q = jnp.bitwise_xor(pos[0], d)
        for f in range(2):
            mz[d][f, 0:4] = col_f[f, pl.ds(4 * q, 4)]
            mz[d][f, 4] = col_d[f]


def place_cols(pos, t, col_s):
    for d in range(4):
        q = jnp.bitwise_xor(pos[0], d)
        for f in range(2):
            col_s[f, pl.ds(4 * q, 4)] = t[d][f]


def col_start(col_s, f):
    return tuple(col_s[f, n] for n in range(N))


def keep_row(f, g, s, row_f, row_d):
    for n in range(N):
        row_f[f, n, 8 * g : 8 * g + 8, :] = s[n]
    row_d[f, 8 * g : 8 * g + 8, :] = s[N]


def row_message(pos, row_f, row_d, mc):
    for d in range(2):
        h = jnp.bitwise_xor(pos[3], d)
        for f in range(2):
            mc[d][f, 0:8] = row_f[f, pl.ds(8 * h, 8)]
            mc[d][f, 8] = row_d[f]


def place_rows(pos, u, row_s):
    for d in range(2):
        h = jnp.bitwise_xor(pos[3], d)
        for f in range(2):
            row_s[f, pl.ds(8 * h, 8)] = u[d][f]


def row_start(row_s, f, g):
    return tuple(row_s[f, n, 8 * g : 8 * g + 8, :] for n in range(N))


def first_kernel(
    pos, pix, win, cw, cb, pw, dtw, dtb, rate, sel,
    hid_rc, hid_cr, conv, delta, sig, proj, bb, mc0, mc1,
    mix, row_f, row_d,
):
    x = pix[...].reshape(10 * 24, C).astype(BF16)
    mix[...] = dot(x, win[:, :E], NN).reshape(10, 24, E)
    acc = jnp.broadcast_to(cb[...].reshape(1, 1, E), (H, W, E))
    for j in range(3):
        for i in range(3):
            acc = acc + mix[i : i + H, j : j + W, :] * cw[3 * i + j].reshape(1, 1, E)
    acc = acc.reshape(H * W, E)
    conv[...] = acc
    hid = acc * sigmoid(acc)
    hid_rc[...] = hid
    cr = permute_tokens(hid, True)
    hid_cr[...] = cr
    for k in range(4):
        pk = mm3(cr if k < 2 else hid, pw[k])
        proj[k] = pk
        if k >= 2:
            spread(pk, sel, bb.at[k - 2])
        zk = mm3(pk, dtw[k]) + dtb[k]
        sig[k] = sigmoid(zk)
        delta[k] = softplus(zk)
    for k in (2, 3):
        for g in (0, 1):
            keep_row(k - 2, g, end_states(k, g, delta, hid_rc, rate, bb), row_f, row_d)
    row_message(pos, row_f, row_d, (mc0, mc1))


def rate_kernel(alog, rate):
    fill_rates(alog, rate)


def col_ends_kernel(
    pos, hid_cr, delta, proj, rate, sel, bb, mz0, mz1, mz2, mz3, col_f, col_d
):
    for k in range(2):
        spread(proj[k], sel, bb.at[k])
    for k in range(2):
        keep_col(k, end_states(k, 0, delta, hid_cr, rate, bb), col_f, col_d)
    col_message(pos, col_f, col_d, (mz0, mz1, mz2, mz3))


def readout_kernel(proj, sel, img, win, cc01, cc23, gate):
    for k in range(4):
        cc = cc01 if k < 2 else cc23
        spread(pltpu.roll(proj[k], 128 - N, 1), sel, cc.at[k % 2])
    gate[...] = dot(img[...], win[:, E:], NN)


def decay(alog, k, n, d):
    r = -jnp.exp(alog[k, n]) * LOG2E
    return jnp.exp2(d * jnp.broadcast_to(r, d.shape))


def row_join_kernel(ks, pos, alog, c0, c1, gy, rc):
    core = pos[3]
    for d, r in enumerate((c0, c1)):
        rc[jnp.bitwise_xor(core, d)] = r[...]
    for f in range(2):
        one, two = (0, 1) if f == 0 else (1, 0)
        for n in range(8):
            gy[f, n] = (
                rc[one, f, n] * decay(alog, ks[2 + f], 8 * core + n, rc[two, f, 8])
                + rc[two, f, n]
            )
        gy[f, 8] = rc[0, f, 8] + rc[1, f, 8]


def join_kernel(ks, pos, alog, r0, r1, r2, r3, g0, g1, mx1, mx2, mx3, my, rs, gx):
    z, x, y, core = pos[0], pos[1], pos[2], pos[3]
    for d, r in enumerate((r0, r1, r2, r3)):
        rs[jnp.bitwise_xor(z, d)] = r[...]
    for f in range(2):
        order = range(4) if f == 0 else range(3, -1, -1)
        for n in range(4):
            total = None
            for t in order:
                piece = rs[t, f, n]
                total = piece if total is None else (
                    total * decay(alog, ks[f], 4 * z + n, rs[t, f, 4]) + piece
                )
            gx[f, n] = total
        gx[f, 4] = rs[0, f, 4] + rs[1, f, 4] + rs[2, f, 4] + rs[3, f, 4]
    for d, m in ((1, mx1), (2, mx2), (3, mx3)):
        m[...] = gx[jnp.where(jnp.bitwise_xor(x, d) > x, 0, 1)]
    f = y >> 1
    mine_first = (y & 1) == f
    own, other = g0[f], g1[f]
    k = jnp.where(f == 0, ks[2], ks[3])
    late = jnp.where(mine_first, other[8], own[8])
    for n in range(8):
        head = jnp.where(mine_first, own[n], other[n])
        tail = jnp.where(mine_first, other[n], own[n])
        my[n] = head * decay(alog, k, 8 * core + n, late) + tail


def start_kernel(
    ks, pos, alog, r0, r1, r2, r3, c0, c1, x1, x2, x3, g1, g2,
    so0, so1, so2, so3, co0, co1, rs, rc, xs, oz, oc,
):
    z, x, y, core = pos[0], pos[1], pos[2], pos[3]
    for d, r in enumerate((r0, r1, r2, r3)):
        rs[jnp.bitwise_xor(z, d)] = r[...]
    for d, r in enumerate((c0, c1)):
        rc[jnp.bitwise_xor(core, d)] = r[...]
    xs[x] = jnp.zeros((5, 8, E), F32)
    for d, r in ((1, x1), (2, x2), (3, x3)):
        xs[jnp.bitwise_xor(x, d)] = r[...]
    for f in range(2):
        order = list(range(4)) if f == 0 else list(range(3, -1, -1))
        for n in range(4):
            s = jnp.zeros((8, E), F32)
            for p in order:
                before = p < x if f == 0 else p > x
                new = s * decay(alog, ks[f], 4 * z + n, xs[p, 4]) + xs[p, n]
                s = jnp.where(before, new, s)
            for t in order:
                oz[t, f, n] = s
                if t != order[-1]:
                    s = s * decay(alog, ks[f], 4 * z + n, rs[t, f, 4]) + rs[t, f, n]
        one, two = (0, 1) if f == 0 else (1, 0)
        far = (y >> 1) == 1 - f
        near = (y & 1) == 1 - f
        for n in range(8):
            s = jnp.where(far, g2[n], 0.0)
            new = s * decay(alog, ks[2 + f], 8 * core + n, g1[f, 8]) + g1[f, n]
            s = jnp.where(near, new, s)
            oc[one, f, n] = s
            oc[two, f, n] = (
                s * decay(alog, ks[2 + f], 8 * core + n, rc[one, f, 8]) + rc[one, f, n]
            )
    for d, o in enumerate((so0, so1, so2, so3)):
        o[...] = oz[jnp.bitwise_xor(z, d)]
    for d, o in enumerate((co0, co1)):
        o[...] = oc[jnp.bitwise_xor(core, d)]


def row_out_kernel(
    pos, u0, u1, hid_rc, delta, rate, bb, cc, yy, row_s,
):
    place_rows(pos, (u0, u1), row_s)
    for k in (2, 3):
        for g in (0, 1):
            outputs(k, g, row_start(row_s, k - 2, g), delta, hid_rc, rate, bb, cc, yy)


def middle_kernel(
    pos, t0, t1, t2, t3, hid_rc, hid_cr, gate, delta, rate, bb, cc, cc23, y23, skip, gain, ow,
    cot,
    gated_out, dgate_out, dtot_rc, dtot_cr, mc0, mc1,
    y01, col_s, row_f, row_d,
):
    place_cols(pos, (t0, t1, t2, t3), col_s)
    for k in range(2):
        outputs(k, 0, col_start(col_s, k), delta, hid_cr, rate, bb, cc, y01)
    skips = skip[0:1] + skip[1:2] + skip[2:3] + skip[3:4]
    total = y23[...] + permute_tokens(y01[...], False) + skips * hid_rc[...]
    centered = total - jnp.mean(total, axis=-1, keepdims=True)
    inv = lax.rsqrt(jnp.mean(centered * centered, axis=-1, keepdims=True) + 1e-05)
    unit = centered * inv
    normed = unit * gain[...]
    gv = gate[...]
    sg = sigmoid(gv)
    act = gv * sg
    gated_out[...] = normed * act
    dgated = dot(cot[...], ow[...], NT)
    dgate_out[...] = dgated * normed * (sg * (1.0 + gv * (1.0 - sg)))
    dn = dgated * act * gain[...]
    dt = inv * (
        dn
        - jnp.mean(dn, axis=-1, keepdims=True)
        - unit * jnp.mean(dn * unit, axis=-1, keepdims=True)
    )
    dtot_rc[...] = dt
    dtot_cr[...] = permute_tokens(dt, True)
    for k in (2, 3):
        for g in (0, 1):
            keep_row(3 - k, g, end_adjoints(k, g, delta, dtot_rc, rate, cc23), row_f, row_d)
    row_message(pos, row_f, row_d, (mc0, mc1))


def side_kernel(gated, dgate, ow, cot, img, win, out, g_out, g_gate, gate_pix):
    gv = gated[...]
    out[...] = mm2(gv, ow[...]).astype(BF16)
    g_out[...] = mm2(gv.T, cot[...])
    dg = dgate[...]
    g_gate[...] = mm2r(img[...].astype(F32).T.astype(BF16), dg)
    gate_pix[...] = mm2(dg, win[:, E:], NT)


def replay_kernel(pos, t0, t1, t2, t3, hid_cr, delta, rate, bb, hist, col_s):
    place_cols(pos, (t0, t1, t2, t3), col_s)
    for k in range(2):
        history(k, 0, col_start(col_s, k), delta, hid_cr, rate, bb, hist.at[k])


def row_replay_kernel(pos, u0, u1, hid_rc, delta, rate, bb, hist, row_s):
    place_rows(pos, (u0, u1), row_s)
    for k in (2, 3):
        for g in (0, 1):
            history(
                k, g, row_start(row_s, k - 2, g), delta, hid_rc, rate, bb,
                hist.at[2 * (k - 2) + g],
            )


def col_back_kernel(pos, delta, dtot_cr, rate, cc, mz0, mz1, mz2, mz3, col_f, col_d):
    for k in range(2):
        keep_col(1 - k, end_adjoints(k, 0, delta, dtot_cr, rate, cc), col_f, col_d)
    col_message(pos, col_f, col_d, (mz0, mz1, mz2, mz3))


def row_grad_kernel(
    pos, v0, v1, hist, hid_rc, delta, sig, rate, bb, cc, dtot_rc, skip, pw, dtw, alog, sel,
    drc, g_a,
    row_b, drate, dx, xb, xc, dz,
):
    place_rows(pos, (v0, v1), row_b)
    drate[...] = jnp.zeros_like(drate)
    for k in (2, 3):
        for g in (0, 1):
            gradients(
                k, g, row_start(row_b, 3 - k, g), delta, sig, hid_rc, dtot_rc, rate, bb, cc,
                hist.at[2 * (k - 2) + g], skip, xb, xc, dz, dx, drate,
            )
    g_a[...] = rate_gradient(drate, alog, 2)
    drc[...] = close_pair(2, dx, dz, xb, xc, dtw, pw, sel)


def last_kernel(
    pos, b0, b1, b2, b3, hist, hid_cr, conv, delta, sig, rate, bb, cc, dtot_cr, drc,
    g_a23, alog, skip, pw, dtw, cw, win, pix, g_out, g_gate, gate_pix, sel,
    msg, center,
    drate, dx, xb, xc, dz, col_b, zpad, gp, edge,
):
    place_cols(pos, (b0, b1, b2, b3), col_b)
    drate[...] = jnp.zeros_like(drate)
    for k in range(2):
        gradients(
            k, 0, col_start(col_b, 1 - k), delta, sig, hid_cr, dtot_cr, rate, bb, cc,
            hist.at[k], skip, xb, xc, dz, dx, drate,
        )
    g_a = jnp.concatenate([rate_gradient(drate, alog, 0), g_a23[...]], axis=0)
    dcr = close_pair(0, dx, dz, xb, xc, dtw, pw, sel)
    dhid = drc[...] + permute_tokens(dcr, False)
    cv = conv[...]
    sg = sigmoid(cv)
    dconv = dhid * (sg * (1.0 + cv * (1.0 - sg)))
    zpad[...] = jnp.zeros_like(zpad)
    zpad[2:10, 8:24, :] = dconv.reshape(H, W, E)
    acc = jnp.zeros((10, 24, E), F32)
    for j in range(3):
        for i in range(3):
            acc = acc + zpad[2 - i : 12 - i, 8 - j : 32 - j, :] * cw[3 * i + j].reshape(1, 1, E)
    flat = acc.reshape(240, E)
    gp[...] = mm2(flat, win[:, :E], NT).reshape(10, 24, C)
    pt = pix[...].reshape(240, C)
    g_in = mm2r(pt.T.astype(BF16), flat)
    center[...] = gate_pix[...] + gp[1:9, 1:17, :].reshape(128, C)
    edge[...] = jnp.zeros_like(edge)
    edge[0:16] = gp[9, 1:17, :]
    edge[16:32] = gp[0, 1:17, :]
    edge[32:40] = gp[1:9, 17, :]
    edge[40:48] = gp[1:9, 0, :]
    edge[48:49] = gp[9, 17:18, :]
    edge[49:50] = gp[9, 0:1, :]
    edge[50:51] = gp[0, 17:18, :]
    edge[51:52] = gp[0, 0:1, :]
    blocks = (
        g_in[:, :128],
        g_in[:, 128:],
        g_gate[:, :128],
        g_gate[:, 128:],
        g_out[:128],
        g_out[128:],
        jnp.concatenate([g_a[:, :128], g_a[:, 128:]], axis=0),
        edge[...].T,
    )
    for b, block in enumerate(blocks):
        msg[pl.ds(b, 128, stride=8), :] = block


def sum_kernel(r, o):
    s = jnp.sum(r[...].reshape(128, 8, 128), axis=0)
    h = r[pl.ds(7, 128, stride=8), :]
    d = lax.broadcasted_iota(jnp.int32, (128, 128), 0)
    i = lax.broadcasted_iota(jnp.int32, (128, 128), 1)
    rr, cc = d >> 4, d & 15
    inn = jnp.zeros((128, 128), F32)
    for lo, hi, dr, dc in (
        (0, 16, -1, 0), (16, 32, 1, 0), (32, 40, 0, -1), (40, 48, 0, 1),
        (48, 49, -1, -1), (49, 50, -1, 1), (50, 51, 1, -1), (51, 52, 1, 1),
    ):
        moved = pltpu.roll(h, (-(dr * 16 + dc)) % 128, 0)
        ok = (i >= lo) & (i < hi)
        ok = ok & (rr + dr >= 0) & (rr + dr < 8) & (cc + dc >= 0) & (cc + dc < 16)
        inn = jnp.where(ok, moved, inn)
    o[...] = jnp.broadcast_to(s[None], (128, 8, 128)).reshape(1024, 128)
    o[pl.ds(7, 128, stride=8), :] = inn


def finish_kernel(q, center, g_pix, g_in, g_out, g_a, acc):
    def block(b):
        return q[pl.ds(b, 128, stride=8), :]

    for b in range(4):
        g_in[:, 128 * b : 128 * b + 128] = block(b)
    g_out[:128] = block(4)
    g_out[128:] = block(5)
    a = block(6)
    g_a[:, :128] = a[:64]
    g_a[:, 128:] = a[64:]
    inn = block(7).T
    acc[...] = center[...].reshape(H, W, C)
    acc[0] = acc[0] + inn[0:16]
    acc[7] = acc[7] + inn[16:32]
    acc[:, 0, :] = acc[:, 0, :] + inn[32:40]
    acc[:, 15, :] = acc[:, 15, :] + inn[40:48]
    acc[0, 0:1, :] = acc[0, 0:1, :] + inn[48:49]
    acc[0, 15:16, :] = acc[0, 15:16, :] + inn[49:50]
    acc[7, 0:1, :] = acc[7, 0:1, :] + inn[50:51]
    acc[7, 15:16, :] = acc[7, 15:16, :] + inn[51:52]
    g_pix[...] = acc[...].reshape(H * W, C).astype(BF16)


def call(kernel, ins, outs, scratch, name, cost=1, after=()):
    vmem = pl.BlockSpec(memory_space=pltpu.VMEM)
    specs = [
        pl.BlockSpec(memory_space=pltpu.SMEM) if x.dtype == jnp.int32 else vmem for x in ins
    ]
    used, extra = len(ins), len(after)

    def body(*refs):
        kernel(*refs[:used], *refs[used + extra :])

    return pl.pallas_call(
        body,
        out_shape=[jax.ShapeDtypeStruct(s, t) for s, t in outs],
        in_specs=specs + [pl.BlockSpec(memory_space=pl.ANY)] * extra,
        out_specs=[vmem] * len(outs),
        scratch_shapes=[pltpu.VMEM(s, F32) for s in scratch],
        compiler_params=pltpu.CompilerParams(vmem_limit_bytes=14 * 1024 * 1024),
        cost_estimate=pl.CostEstimate(
            flops=0, bytes_accessed=cost * 3_500_000, transcendentals=0
        ),
        name=name,
    )(*ins, *after)


def xor_permute(x, axis, mask):
    return lax.ppermute(x, axis, [(i, i ^ mask) for i in range(lax.axis_size(axis))])


def exchange(pos, alog4, mz, mc, ks, after=((), ())):
    r = [mz[0]] + [xor_permute(mz[d], "col", d) for d in range(1, 4)]
    c = [mc[0], xor_permute(mc[1], "row", 1)]
    (g0,) = call(
        partial(row_join_kernel, ks), [pos, alog4] + c, [((2, 9, 16, E), F32)],
        [(2, 2, 9, 16, E)], "row_join", 1, (mz[0],),
    )
    g1 = xor_permute(g0, "row", 2)
    m = call(
        partial(join_kernel, ks), [pos, alog4] + r + [g0, g1],
        [((5, 8, E), F32)] * 3 + [((8, 16, E), F32)],
        [(4, 2, 5, 8, E), (2, 5, 8, E)], "join", 1, after[0],
    )
    g2 = xor_permute(m[3], "row", 4)
    xm = [xor_permute(m[d - 1], "col", 4 * d) for d in range(1, 4)]
    s = call(
        partial(start_kernel, ks), [pos, alog4] + r + c + xm + [g1, g2],
        [((2, 4, 8, E), F32)] * 4 + [((2, 8, 16, E), F32)] * 2,
        [(4, 2, 5, 8, E), (2, 2, 9, 16, E), (4, 5, 8, E), (4, 2, 4, 8, E), (2, 2, 8, 16, E)],
        "starts", 1, after[1],
    )
    t = [s[0]] + [xor_permute(s[d], "col", d) for d in range(1, 4)]
    u = [s[4], xor_permute(s[5], "row", 1)]
    return t, u


def rims(head, tail, axis):
    count = lax.axis_size(axis)
    mine = lax.axis_index(axis)
    odd = mine % 2 == 1
    near = xor_permute(jnp.where(odd, head, tail), axis, 1)
    pairs = [(i, (i + 1 if i % 2 == 1 else i - 1) % count) for i in range(count)]
    far = lax.ppermute(jnp.where(odd, tail, head), axis, pairs)
    before = jnp.where(mine == 0, 0.0, jnp.where(odd, near, far))
    after = jnp.where(mine == count - 1, 0.0, jnp.where(odd, far, near))
    return before, after


def per_device(
    image, in_weight, conv_weight, conv_bias, proj_weight, dt_weight, dt_bias, a_log,
    skip_gain, norm_gain, out_weight, cotangent,
):
    r, c = lax.axis_index("row"), lax.axis_index("col")
    pos = jnp.stack([c % 4, c // 4, r // 2, r % 2]).astype(jnp.int32)
    wide = image.astype(F32)
    up, down = rims(wide[:1], wide[H - 1 :], "row")
    tall = jnp.concatenate([up, wide, down], axis=0)
    left, right = rims(tall[:, :1], tall[:, W - 1 :], "col")
    pix = jnp.concatenate([left, tall, right, jnp.zeros((H + 2, 6, C), F32)], axis=1)
    img = image.reshape(H * W, C)
    cot = cotangent.reshape(H * W, C)
    cw = conv_weight.reshape(9, 1, E)
    cb = conv_bias.reshape(1, E)
    pw = jnp.pad(proj_weight, ((0, 0), (0, 0), (0, 88)))
    dtw = jnp.pad(dt_weight, ((0, 0), (0, 120), (0, 0)))
    entry = lax.broadcasted_iota(jnp.int32, (256, N * 128), 0) & 127
    state = lax.broadcasted_iota(jnp.int32, (256, N * 128), 1) >> 7
    sel = jnp.where(entry == state + 8, 1.0, 0.0).astype(BF16)
    dtb = dt_bias.reshape(4, 1, E)
    alog = a_log.reshape(4 * N, E)
    alog4 = a_log.reshape(4, N, 1, E)
    gain = norm_gain.reshape(1, E)

    tok = ((H * W, E), F32)
    four = (4, H * W, E)
    two = (2, H * W, E)
    rates = (4 * N, 8, E)
    prj = (4, H * W, 128)
    spreads = (2, H * W, N * 128)
    rows = [(2, N, 16, E), (2, 16, E)]
    cols = [(2, N, 8, E), (2, 8, E)]
    mcs = [((2, 9, 16, E), F32)] * 2
    mzs = [((2, 5, 8, E), F32)] * 4
    (rate,) = call(rate_kernel, [alog], [(rates, F32)], [], "rates", 1)
    hid_rc, hid_cr, conv, delta, sig, proj, bb23, *mc = call(
        first_kernel,
        [pos, pix, in_weight, cw, cb, pw, dtw, dtb, rate, sel],
        [tok, tok, tok, (four, F32), (four, F32), (prj, F32), (spreads, F32)] + mcs,
        [(10, 24, E)] + rows, "first", 4,
    )
    bb01, *mz = call(
        col_ends_kernel, [pos, hid_cr, delta, proj, rate, sel], [(spreads, F32)] + mzs, cols,
        "col_ends", 2,
    )
    cc01, cc23, gate = call(
        readout_kernel, [proj, sel, img, in_weight], [(spreads, F32), (spreads, F32), tok], [],
        "readout", 1,
    )
    t, u = exchange(pos, alog4, mz, mc, (0, 1, 2, 3), ((), (cc01,)))
    (y23,) = call(
        row_out_kernel, [pos] + u + [hid_rc, delta, rate, bb23, cc23],
        [tok], rows[:1], "row_out", 3,
    )
    gated, dgate, dtot_rc, dtot_cr, *mc = call(
        middle_kernel,
        [pos] + t + [hid_rc, hid_cr, gate, delta, rate, bb01, cc01, cc23, y23, skip_gain, gain,
                     out_weight, cot],
        [tok, tok, tok, tok] + mcs,
        [tok[0]] + cols[:1] + rows, "middle", 5,
    )
    mz = call(
        col_back_kernel, [pos, delta, dtot_cr, rate, cc01], mzs, cols, "col_back", 2
    )
    out, g_out, g_gate, gate_pix = call(
        side_kernel, [gated, dgate, out_weight, cot, img, in_weight],
        [((H * W, C), BF16), ((E, C), F32), ((C, E), F32), ((H * W, C), F32)], [], "side", 1,
    )
    (hist01,) = call(
        replay_kernel, [pos] + t + [hid_cr, delta, rate, bb01],
        [((2, W + 1, N, 8, E), F32)], cols[:1], "replay", 2,
    )
    (hist23,) = call(
        row_replay_kernel, [pos] + u + [hid_rc, delta, rate, bb23],
        [((4, H + 1, N, 8, E), F32)], rows[:1], "row_replay", 2,
    )
    b, v = exchange(pos, alog4, mz, mc, (1, 0, 3, 2), ((hist23, g_out), (hist01,)))
    work = [(2 * N, 8, E), tok[0], spreads, spreads, two]
    drc, g_a23 = call(
        row_grad_kernel,
        [pos] + v + [hist23, hid_rc, delta, sig, rate, bb23, cc23, dtot_rc, skip_gain, pw, dtw,
                     alog, sel],
        [tok, ((2 * N, E), F32)],
        [rows[0]] + work, "row_grad", 7,
    )
    msg, center = call(
        last_kernel,
        [pos] + b + [hist01, hid_cr, conv, delta, sig, rate, bb01, cc01, dtot_cr, drc, g_a23,
                     alog, skip_gain, pw, dtw, cw, in_weight, pix, g_out, g_gate, gate_pix, sel],
        [((1024, 128), F32), ((H * W, C), F32)],
        work + [cols[0], (12, 32, E), (10, 24, C), (128, 128)],
        "last", 8,
    )
    got = lax.all_to_all(msg.reshape(128, 8, 128), AXES, 0, 0, tiled=True)
    (back,) = call(sum_kernel, [got.reshape(1024, 128)], [((1024, 128), F32)], [], "sum")
    got = lax.all_to_all(back.reshape(128, 8, 128), AXES, 0, 0, tiled=True)
    g_pix, g_in, g_outw, g_a = call(
        finish_kernel, [got.reshape(1024, 128), center],
        [((H * W, C), BF16), ((C, 2 * E), F32), ((E, C), F32), ((4 * N, E), F32)],
        [(H, W, C)], "finish",
    )
    return (
        out.reshape(H, W, C), g_pix.reshape(H, W, C), g_in, g_outw, g_a.reshape(4, N, E),
    )


def solution(mesh):
    tile = P("row", "col", None)
    return jax.shard_map(
        per_device,
        mesh=mesh,
        in_specs=(tile,) + (P(),) * 10 + (tile,),
        out_specs=(tile, tile, P(), P(), P()),
        check_vma=False,
    )
```

```python
from functools import partial

import jax
import jax.numpy as jnp
from jax import lax
from jax.experimental import pallas as pl
from jax.experimental.pallas import tpu as pltpu
from jax.sharding import PartitionSpec as P

F32 = jnp.float32
BF16 = jnp.bfloat16
H, W, C, E, N = 8, 16, 128, 256, 16
LOG2E = 1.4426950408889634
LN2 = 0.6931471805599453
AXES = ("row", "col")


def split2(a):
    hi = a.astype(BF16)
    return hi, (a - hi.astype(F32)).astype(BF16)


def dot(a, b, dims):
    return lax.dot_general(a, b, (dims, ((), ())), preferred_element_type=F32)


NN = ((1,), (0,))
NT = ((1,), (1,))


def mm3(a, b, dims=NN):
    ah, al = split2(a)
    bh, bl = split2(b)
    return dot(ah, bh, dims) + (dot(ah, bl, dims) + dot(al, bh, dims))


def mm2(a, b, dims=NN):
    ah, al = split2(a)
    return dot(ah, b, dims) + dot(al, b, dims)


def mm2r(a, b, dims=NN):
    bh, bl = split2(b)
    return dot(a, bh, dims) + dot(a, bl, dims)


def permute_tokens(x, to_cr):
    o = lax.broadcasted_iota(jnp.int32, (128, 128), 0)
    i = lax.broadcasted_iota(jnp.int32, (128, 128), 1)
    if to_cr:
        hit = i == ((o & 7) * 16 + (o >> 3))
    else:
        hit = i == ((o & 15) * 8 + (o >> 4))
    m = jnp.where(hit, 1.0, 0.0).astype(BF16)
    hi = x.astype(BF16)
    rest = x - hi.astype(F32)
    mid = rest.astype(BF16)
    low = (rest - mid.astype(F32)).astype(BF16)
    return dot(m, hi, NN) + (dot(m, mid, NN) + dot(m, low, NN))


def softplus(z):
    return jnp.maximum(z, 0.0) + jnp.log1p(jnp.exp(-jnp.abs(z)))


def sigmoid(v):
    return 1.0 / (1.0 + jnp.exp(-v))


def spread(p, sel, dst):
    hi, lo = split2(p)
    dst[...] = dot(jnp.concatenate([hi, lo], axis=1), sel[...], NN)


def lanes(ref, k, at, n):
    v = ref[k, at, 128 * n : 128 * n + 128]
    return jnp.concatenate([v, v], axis=1)


def fold(v):
    return v[:, :128] + v[:, 128:]


def fill_rates(alog, rate):
    r = -jnp.exp(alog[...]) * LOG2E
    for i in range(4 * N):
        rate[i] = jnp.broadcast_to(r[i : i + 1], (8, E))


def steps(k):
    return W if k < 2 else H


def groups(k):
    return (0,) if k < 2 else (0, 1)


def row_at(k, g, i):
    t = i if k % 2 == 0 else steps(k) - 1 - i
    start = t * 8 if k < 2 else t * 16 + g * 8
    return pl.multiple_of(start, 8)


def end_states(k, g, delta, h, rate, bb):
    def body(i, s):
        at = pl.ds(row_at(k, g, i), 8)
        d = delta[k, at, :]
        u = d * h[at, :]
        new = [
            jnp.exp2(d * rate[k * N + n]) * s[n] + u * lanes(bb, k % 2, at, n) for n in range(N)
        ]
        return tuple(new) + (s[N] + d,)

    return lax.fori_loop(0, steps(k), body, (jnp.zeros((8, E), F32),) * (N + 1))


def outputs(k, g, start, delta, h, rate, bb, cc, yy):
    def body(i, s):
        at = pl.ds(row_at(k, g, i), 8)
        d = delta[k, at, :]
        u = d * h[at, :]
        y = None
        new = []
        for n in range(N):
            v = jnp.exp2(d * rate[k * N + n]) * s[n] + u * lanes(bb, k % 2, at, n)
            new.append(v)
            c = v * lanes(cc, k % 2, at, n)
            y = c if y is None else y + c
        yy[at, :] = y if k % 2 == 0 else yy[at, :] + y
        return tuple(new)

    lax.fori_loop(0, steps(k), body, start)


def end_adjoints(k, g, delta, dy, rate, cc):
    def body(j, s):
        at = pl.ds(row_at(k, g, steps(k) - 1 - j), 8)
        d = delta[k, at, :]
        t = dy[at, :]
        new = [
            jnp.exp2(d * rate[k * N + n]) * (s[n] + t * lanes(cc, k % 2, at, n))
            for n in range(N)
        ]
        return tuple(new) + (s[N] + d,)

    return lax.fori_loop(0, steps(k), body, (jnp.zeros((8, E), F32),) * (N + 1))


def history(k, g, start, delta, h, rate, bb, hist, dy, xc):
    def body(i, s):
        at = pl.ds(row_at(k, g, i), 8)
        d = delta[k, at, :]
        u = d * h[at, :]
        t = dy[at, :]
        new = []
        for n in range(N):
            hist[i, n] = s[n]
            v = jnp.exp2(d * rate[k * N + n]) * s[n] + u * lanes(bb, k % 2, at, n)
            new.append(v)
            xc[k % 2, at, 128 * n : 128 * n + 128] = fold(t * v)
        return tuple(new)

    lax.fori_loop(0, steps(k), body, start)


def readout_gradient(xc, sel, dpc):
    for kk in range(2):
        dpc[kk] = pltpu.roll(mm2(xc[kk], sel[0:128, :], NT), N, 1)


def gradients(k, g, end, delta, sig, h, dy, rate, bb, cc, hist, skip, xb, dz, dx, drate):
    kk = k % 2

    def body(j, m):
        i = steps(k) - 1 - j
        at = pl.ds(row_at(k, g, i), 8)
        d = delta[k, at, :]
        xx = h[at, :]
        u = d * xx
        t = dy[at, :]
        du = jnp.zeros((8, E), F32)
        dd = jnp.zeros((8, E), F32)
        new = []
        for n in range(N):
            r = rate[k * N + n]
            lam = lanes(cc, kk, at, n) * t + m[n]
            out = jnp.exp2(d * r) * lam
            new.append(out)
            xb[kk, at, 128 * n : 128 * n + 128] = fold(lam * u)
            du = du + lam * lanes(bb, kk, at, n)
            q = out * hist[i, n]
            dd = dd + q * r
            drate[kk * N + n] = drate[kk * N + n] + q * d
        dz[kk, at, :] = (du * xx + dd * LN2) * sig[k, at, :]
        dxv = du * d + skip[k : k + 1] * t
        dx[at, :] = dxv if kk == 0 else dx[at, :] + dxv
        return tuple(new)

    lax.fori_loop(0, steps(k), body, end)


def close_pair(first, dx, dz, xb, dpc, dtw, pw, sel):
    total = dx[...]
    pick = sel[0:128, :]
    for kk in range(2):
        dp = (
            mm3(dz[kk], dtw[first + kk], NT) + mm2(xb[kk], pick, NT) + dpc[kk]
        )
        total = total + mm3(dp, pw[first + kk], NT)
    return total


def rate_gradient(drate, alog, first):
    return jnp.sum(drate[...], axis=1) * (-jnp.exp(alog[N * first : N * first + 2 * N]))


def keep_col(f, s, col_f, col_d):
    for n in range(N):
        col_f[f, n] = s[n]
    col_d[f] = s[N]


def col_message(pos, col_f, col_d, mz):
    for d in range(4):
        q = jnp.bitwise_xor(pos[0], d)
        for f in range(2):
            mz[d][f, 0:4] = col_f[f, pl.ds(4 * q, 4)]
            mz[d][f, 4] = col_d[f]


def place_cols(pos, t, col_s):
    for d in range(4):
        q = jnp.bitwise_xor(pos[0], d)
        for f in range(2):
            col_s[f, pl.ds(4 * q, 4)] = t[d][f]


def col_start(col_s, f):
    return tuple(col_s[f, n] for n in range(N))


def keep_row(f, g, s, row_f, row_d):
    for n in range(N):
        row_f[f, n, 8 * g : 8 * g + 8, :] = s[n]
    row_d[f, 8 * g : 8 * g + 8, :] = s[N]


def row_message(pos, row_f, row_d, mc):
    for d in range(2):
        h = jnp.bitwise_xor(pos[3], d)
        for f in range(2):
            mc[d][f, 0:8] = row_f[f, pl.ds(8 * h, 8)]
            mc[d][f, 8] = row_d[f]


def place_rows(pos, u, row_s):
    for d in range(2):
        h = jnp.bitwise_xor(pos[3], d)
        for f in range(2):
            row_s[f, pl.ds(8 * h, 8)] = u[d][f]


def row_start(row_s, f, g):
    return tuple(row_s[f, n, 8 * g : 8 * g + 8, :] for n in range(N))


def first_kernel(
    pos, pix, win, cw, cb, pw, dtw, dtb, rate, sel,
    hid_rc, hid_cr, conv, delta, sig, proj, bb, mc0, mc1,
    mix, row_f, row_d,
):
    x = pix[...].reshape(10 * 24, C).astype(BF16)
    mix[...] = dot(x, win[:, :E], NN).reshape(10, 24, E)
    acc = jnp.broadcast_to(cb[...].reshape(1, 1, E), (H, W, E))
    for j in range(3):
        for i in range(3):
            acc = acc + mix[i : i + H, j : j + W, :] * cw[3 * i + j].reshape(1, 1, E)
    acc = acc.reshape(H * W, E)
    conv[...] = acc
    hid = acc * sigmoid(acc)
    hid_rc[...] = hid
    cr = permute_tokens(hid, True)
    hid_cr[...] = cr
    for k in range(4):
        pk = mm3(cr if k < 2 else hid, pw[k])
        proj[k] = pk
        if k >= 2:
            spread(pk, sel, bb.at[k - 2])
        zk = mm3(pk, dtw[k]) + dtb[k]
        sig[k] = sigmoid(zk)
        delta[k] = softplus(zk)
    for k in (2, 3):
        for g in (0, 1):
            keep_row(k - 2, g, end_states(k, g, delta, hid_rc, rate, bb), row_f, row_d)
    row_message(pos, row_f, row_d, (mc0, mc1))


def rate_kernel(alog, rate):
    fill_rates(alog, rate)


def col_ends_kernel(
    pos, hid_cr, delta, proj, rate, sel, bb, mz0, mz1, mz2, mz3, col_f, col_d
):
    for k in range(2):
        spread(proj[k], sel, bb.at[k])
    for k in range(2):
        keep_col(k, end_states(k, 0, delta, hid_cr, rate, bb), col_f, col_d)
    col_message(pos, col_f, col_d, (mz0, mz1, mz2, mz3))


def readout_kernel(proj, sel, img, win, cc01, cc23, gate):
    for k in range(4):
        cc = cc01 if k < 2 else cc23
        spread(pltpu.roll(proj[k], 128 - N, 1), sel, cc.at[k % 2])
    gate[...] = dot(img[...], win[:, E:], NN)


def decay(alog, k, n, d):
    r = -jnp.exp(alog[k, n]) * LOG2E
    return jnp.exp2(d * jnp.broadcast_to(r, d.shape))


def row_join_kernel(ks, pos, alog, c0, c1, gy, rc):
    core = pos[3]
    for d, r in enumerate((c0, c1)):
        rc[jnp.bitwise_xor(core, d)] = r[...]
    for f in range(2):
        one, two = (0, 1) if f == 0 else (1, 0)
        for n in range(8):
            gy[f, n] = (
                rc[one, f, n] * decay(alog, ks[2 + f], 8 * core + n, rc[two, f, 8])
                + rc[two, f, n]
            )
        gy[f, 8] = rc[0, f, 8] + rc[1, f, 8]


def join_kernel(ks, pos, alog, r0, r1, r2, r3, g0, g1, mx1, mx2, mx3, my, rs, gx):
    z, x, y, core = pos[0], pos[1], pos[2], pos[3]
    for d, r in enumerate((r0, r1, r2, r3)):
        rs[jnp.bitwise_xor(z, d)] = r[...]
    for f in range(2):
        order = range(4) if f == 0 else range(3, -1, -1)
        for n in range(4):
            total = None
            for t in order:
                piece = rs[t, f, n]
                total = piece if total is None else (
                    total * decay(alog, ks[f], 4 * z + n, rs[t, f, 4]) + piece
                )
            gx[f, n] = total
        gx[f, 4] = rs[0, f, 4] + rs[1, f, 4] + rs[2, f, 4] + rs[3, f, 4]
    for d, m in ((1, mx1), (2, mx2), (3, mx3)):
        m[...] = gx[jnp.where(jnp.bitwise_xor(x, d) > x, 0, 1)]
    f = y >> 1
    mine_first = (y & 1) == f
    own, other = g0[f], g1[f]
    k = jnp.where(f == 0, ks[2], ks[3])
    late = jnp.where(mine_first, other[8], own[8])
    for n in range(8):
        head = jnp.where(mine_first, own[n], other[n])
        tail = jnp.where(mine_first, other[n], own[n])
        my[n] = head * decay(alog, k, 8 * core + n, late) + tail


def start_kernel(
    ks, pos, alog, r0, r1, r2, r3, c0, c1, x1, x2, x3, g1, g2,
    so0, so1, so2, so3, co0, co1, rs, rc, xs, oz, oc,
):
    z, x, y, core = pos[0], pos[1], pos[2], pos[3]
    for d, r in enumerate((r0, r1, r2, r3)):
        rs[jnp.bitwise_xor(z, d)] = r[...]
    for d, r in enumerate((c0, c1)):
        rc[jnp.bitwise_xor(core, d)] = r[...]
    xs[x] = jnp.zeros((5, 8, E), F32)
    for d, r in ((1, x1), (2, x2), (3, x3)):
        xs[jnp.bitwise_xor(x, d)] = r[...]
    for f in range(2):
        order = list(range(4)) if f == 0 else list(range(3, -1, -1))
        for n in range(4):
            s = jnp.zeros((8, E), F32)
            for p in order:
                before = p < x if f == 0 else p > x
                new = s * decay(alog, ks[f], 4 * z + n, xs[p, 4]) + xs[p, n]
                s = jnp.where(before, new, s)
            for t in order:
                oz[t, f, n] = s
                if t != order[-1]:
                    s = s * decay(alog, ks[f], 4 * z + n, rs[t, f, 4]) + rs[t, f, n]
        one, two = (0, 1) if f == 0 else (1, 0)
        far = (y >> 1) == 1 - f
        near = (y & 1) == 1 - f
        for n in range(8):
            s = jnp.where(far, g2[n], 0.0)
            new = s * decay(alog, ks[2 + f], 8 * core + n, g1[f, 8]) + g1[f, n]
            s = jnp.where(near, new, s)
            oc[one, f, n] = s
            oc[two, f, n] = (
                s * decay(alog, ks[2 + f], 8 * core + n, rc[one, f, 8]) + rc[one, f, n]
            )
    for d, o in enumerate((so0, so1, so2, so3)):
        o[...] = oz[jnp.bitwise_xor(z, d)]
    for d, o in enumerate((co0, co1)):
        o[...] = oc[jnp.bitwise_xor(core, d)]


def row_out_kernel(
    pos, u0, u1, hid_rc, delta, rate, bb, cc, yy, row_s,
):
    place_rows(pos, (u0, u1), row_s)
    for k in (2, 3):
        for g in (0, 1):
            outputs(k, g, row_start(row_s, k - 2, g), delta, hid_rc, rate, bb, cc, yy)


def middle_kernel(
    pos, t0, t1, t2, t3, hid_rc, hid_cr, gate, delta, rate, bb, cc, cc23, y23, skip, gain, ow,
    cot,
    gated_out, dgate_out, dtot_rc, dtot_cr, mc0, mc1,
    y01, col_s, row_f, row_d,
):
    place_cols(pos, (t0, t1, t2, t3), col_s)
    for k in range(2):
        outputs(k, 0, col_start(col_s, k), delta, hid_cr, rate, bb, cc, y01)
    skips = skip[0:1] + skip[1:2] + skip[2:3] + skip[3:4]
    total = y23[...] + permute_tokens(y01[...], False) + skips * hid_rc[...]
    centered = total - jnp.mean(total, axis=-1, keepdims=True)
    inv = lax.rsqrt(jnp.mean(centered * centered, axis=-1, keepdims=True) + 1e-05)
    unit = centered * inv
    normed = unit * gain[...]
    gv = gate[...]
    sg = sigmoid(gv)
    act = gv * sg
    gated_out[...] = normed * act
    dgated = dot(cot[...], ow[...], NT)
    dgate_out[...] = dgated * normed * (sg * (1.0 + gv * (1.0 - sg)))
    dn = dgated * act * gain[...]
    dt = inv * (
        dn
        - jnp.mean(dn, axis=-1, keepdims=True)
        - unit * jnp.mean(dn * unit, axis=-1, keepdims=True)
    )
    dtot_rc[...] = dt
    dtot_cr[...] = permute_tokens(dt, True)
    for k in (2, 3):
        for g in (0, 1):
            keep_row(3 - k, g, end_adjoints(k, g, delta, dtot_rc, rate, cc23), row_f, row_d)
    row_message(pos, row_f, row_d, (mc0, mc1))


def side_kernel(gated, dgate, ow, cot, img, win, out, g_out, g_gate, gate_pix):
    gv = gated[...]
    out[...] = mm2(gv, ow[...]).astype(BF16)
    g_out[...] = mm2(gv.T, cot[...])
    dg = dgate[...]
    g_gate[...] = mm2r(img[...].astype(F32).T.astype(BF16), dg)
    gate_pix[...] = mm2(dg, win[:, E:], NT)


def replay_kernel(
    pos, t0, t1, t2, t3, hid_cr, delta, rate, bb, dy, sel, hist, dpc, col_s, xc
):
    place_cols(pos, (t0, t1, t2, t3), col_s)
    for k in range(2):
        history(k, 0, col_start(col_s, k), delta, hid_cr, rate, bb, hist.at[k], dy, xc)
    readout_gradient(xc, sel, dpc)


def row_replay_kernel(pos, u0, u1, hid_rc, delta, rate, bb, dy, sel, hist, dpc, row_s, xc):
    place_rows(pos, (u0, u1), row_s)
    for k in (2, 3):
        for g in (0, 1):
            history(
                k, g, row_start(row_s, k - 2, g), delta, hid_rc, rate, bb,
                hist.at[2 * (k - 2) + g], dy, xc,
            )
    readout_gradient(xc, sel, dpc)


def col_back_kernel(pos, delta, dtot_cr, rate, cc, mz0, mz1, mz2, mz3, col_f, col_d):
    for k in range(2):
        keep_col(1 - k, end_adjoints(k, 0, delta, dtot_cr, rate, cc), col_f, col_d)
    col_message(pos, col_f, col_d, (mz0, mz1, mz2, mz3))


def row_grad_kernel(
    pos, v0, v1, hist, dpc, hid_rc, delta, sig, rate, bb, cc, dtot_rc, skip, pw, dtw, alog, sel,
    drc, g_a,
    row_b, drate, dx, xb, dz,
):
    place_rows(pos, (v0, v1), row_b)
    drate[...] = jnp.zeros_like(drate)
    for k in (2, 3):
        for g in (0, 1):
            gradients(
                k, g, row_start(row_b, 3 - k, g), delta, sig, hid_rc, dtot_rc, rate, bb, cc,
                hist.at[2 * (k - 2) + g], skip, xb, dz, dx, drate,
            )
    g_a[...] = rate_gradient(drate, alog, 2)
    drc[...] = close_pair(2, dx, dz, xb, dpc, dtw, pw, sel)


def last_kernel(
    pos, b0, b1, b2, b3, hist, dpc, hid_cr, conv, delta, sig, rate, bb, cc, dtot_cr, drc,
    g_a23, alog, skip, pw, dtw, cw, win, pix, g_out, g_gate, gate_pix, sel,
    msg, center,
    drate, dx, xb, dz, col_b, zpad, gp, edge,
):
    place_cols(pos, (b0, b1, b2, b3), col_b)
    drate[...] = jnp.zeros_like(drate)
    for k in range(2):
        gradients(
            k, 0, col_start(col_b, 1 - k), delta, sig, hid_cr, dtot_cr, rate, bb, cc,
            hist.at[k], skip, xb, dz, dx, drate,
        )
    g_a = jnp.concatenate([rate_gradient(drate, alog, 0), g_a23[...]], axis=0)
    dcr = close_pair(0, dx, dz, xb, dpc, dtw, pw, sel)
    dhid = drc[...] + permute_tokens(dcr, False)
    cv = conv[...]
    sg = sigmoid(cv)
    dconv = dhid * (sg * (1.0 + cv * (1.0 - sg)))
    zpad[...] = jnp.zeros_like(zpad)
    zpad[2:10, 8:24, :] = dconv.reshape(H, W, E)
    acc = jnp.zeros((10, 24, E), F32)
    for j in range(3):
        for i in range(3):
            acc = acc + zpad[2 - i : 12 - i, 8 - j : 32 - j, :] * cw[3 * i + j].reshape(1, 1, E)
    flat = acc.reshape(240, E)
    gp[...] = mm2(flat, win[:, :E], NT).reshape(10, 24, C)
    pt = pix[...].reshape(240, C)
    g_in = mm2r(pt.T.astype(BF16), flat)
    center[...] = gate_pix[...] + gp[1:9, 1:17, :].reshape(128, C)
    edge[...] = jnp.zeros_like(edge)
    edge[0:16] = gp[9, 1:17, :]
    edge[16:32] = gp[0, 1:17, :]
    edge[32:40] = gp[1:9, 17, :]
    edge[40:48] = gp[1:9, 0, :]
    edge[48:49] = gp[9, 17:18, :]
    edge[49:50] = gp[9, 0:1, :]
    edge[50:51] = gp[0, 17:18, :]
    edge[51:52] = gp[0, 0:1, :]
    blocks = (
        g_in[:, :128],
        g_in[:, 128:],
        g_gate[:, :128],
        g_gate[:, 128:],
        g_out[:128],
        g_out[128:],
        jnp.concatenate([g_a[:, :128], g_a[:, 128:]], axis=0),
        edge[...].T,
    )
    for b, block in enumerate(blocks):
        msg[pl.ds(b, 128, stride=8), :] = block


def sum_kernel(r, o):
    s = jnp.sum(r[...].reshape(128, 8, 128), axis=0)
    h = r[pl.ds(7, 128, stride=8), :]
    d = lax.broadcasted_iota(jnp.int32, (128, 128), 0)
    i = lax.broadcasted_iota(jnp.int32, (128, 128), 1)
    rr, cc = d >> 4, d & 15
    inn = jnp.zeros((128, 128), F32)
    for lo, hi, dr, dc in (
        (0, 16, -1, 0), (16, 32, 1, 0), (32, 40, 0, -1), (40, 48, 0, 1),
        (48, 49, -1, -1), (49, 50, -1, 1), (50, 51, 1, -1), (51, 52, 1, 1),
    ):
        moved = pltpu.roll(h, (-(dr * 16 + dc)) % 128, 0)
        ok = (i >= lo) & (i < hi)
        ok = ok & (rr + dr >= 0) & (rr + dr < 8) & (cc + dc >= 0) & (cc + dc < 16)
        inn = jnp.where(ok, moved, inn)
    o[...] = jnp.broadcast_to(s[None], (128, 8, 128)).reshape(1024, 128)
    o[pl.ds(7, 128, stride=8), :] = inn


def finish_kernel(q, center, g_pix, g_in, g_out, g_a, acc):
    def block(b):
        return q[pl.ds(b, 128, stride=8), :]

    for b in range(4):
        g_in[:, 128 * b : 128 * b + 128] = block(b)
    g_out[:128] = block(4)
    g_out[128:] = block(5)
    a = block(6)
    g_a[:, :128] = a[:64]
    g_a[:, 128:] = a[64:]
    inn = block(7).T
    acc[...] = center[...].reshape(H, W, C)
    acc[0] = acc[0] + inn[0:16]
    acc[7] = acc[7] + inn[16:32]
    acc[:, 0, :] = acc[:, 0, :] + inn[32:40]
    acc[:, 15, :] = acc[:, 15, :] + inn[40:48]
    acc[0, 0:1, :] = acc[0, 0:1, :] + inn[48:49]
    acc[0, 15:16, :] = acc[0, 15:16, :] + inn[49:50]
    acc[7, 0:1, :] = acc[7, 0:1, :] + inn[50:51]
    acc[7, 15:16, :] = acc[7, 15:16, :] + inn[51:52]
    g_pix[...] = acc[...].reshape(H * W, C).astype(BF16)


def call(kernel, ins, outs, scratch, name, cost=1, after=()):
    vmem = pl.BlockSpec(memory_space=pltpu.VMEM)
    specs = [
        pl.BlockSpec(memory_space=pltpu.SMEM) if x.dtype == jnp.int32 else vmem for x in ins
    ]
    used, extra = len(ins), len(after)

    def body(*refs):
        kernel(*refs[:used], *refs[used + extra :])

    return pl.pallas_call(
        body,
        out_shape=[jax.ShapeDtypeStruct(s, t) for s, t in outs],
        in_specs=specs + [pl.BlockSpec(memory_space=pl.ANY)] * extra,
        out_specs=[vmem] * len(outs),
        scratch_shapes=[pltpu.VMEM(s, F32) for s in scratch],
        compiler_params=pltpu.CompilerParams(vmem_limit_bytes=14 * 1024 * 1024),
        cost_estimate=pl.CostEstimate(
            flops=0, bytes_accessed=cost * 3_500_000, transcendentals=0
        ),
        name=name,
    )(*ins, *after)


def xor_permute(x, axis, mask):
    return lax.ppermute(x, axis, [(i, i ^ mask) for i in range(lax.axis_size(axis))])


def exchange(pos, alog4, mz, mc, ks, after=((), ())):
    r = [mz[0]] + [xor_permute(mz[d], "col", d) for d in range(1, 4)]
    c = [mc[0], xor_permute(mc[1], "row", 1)]
    (g0,) = call(
        partial(row_join_kernel, ks), [pos, alog4] + c, [((2, 9, 16, E), F32)],
        [(2, 2, 9, 16, E)], "row_join", 1, (mz[0],),
    )
    g1 = xor_permute(g0, "row", 2)
    m = call(
        partial(join_kernel, ks), [pos, alog4] + r + [g0, g1],
        [((5, 8, E), F32)] * 3 + [((8, 16, E), F32)],
        [(4, 2, 5, 8, E), (2, 5, 8, E)], "join", 1, after[0],
    )
    g2 = xor_permute(m[3], "row", 4)
    xm = [xor_permute(m[d - 1], "col", 4 * d) for d in range(1, 4)]
    s = call(
        partial(start_kernel, ks), [pos, alog4] + r + c + xm + [g1, g2],
        [((2, 4, 8, E), F32)] * 4 + [((2, 8, 16, E), F32)] * 2,
        [(4, 2, 5, 8, E), (2, 2, 9, 16, E), (4, 5, 8, E), (4, 2, 4, 8, E), (2, 2, 8, 16, E)],
        "starts", 1, after[1],
    )
    t = [s[0]] + [xor_permute(s[d], "col", d) for d in range(1, 4)]
    u = [s[4], xor_permute(s[5], "row", 1)]
    return t, u


def rims(head, tail, axis):
    count = lax.axis_size(axis)
    mine = lax.axis_index(axis)
    odd = mine % 2 == 1
    near = xor_permute(jnp.where(odd, head, tail), axis, 1)
    pairs = [(i, (i + 1 if i % 2 == 1 else i - 1) % count) for i in range(count)]
    far = lax.ppermute(jnp.where(odd, tail, head), axis, pairs)
    before = jnp.where(mine == 0, 0.0, jnp.where(odd, near, far))
    after = jnp.where(mine == count - 1, 0.0, jnp.where(odd, far, near))
    return before, after


def per_device(
    image, in_weight, conv_weight, conv_bias, proj_weight, dt_weight, dt_bias, a_log,
    skip_gain, norm_gain, out_weight, cotangent,
):
    r, c = lax.axis_index("row"), lax.axis_index("col")
    pos = jnp.stack([c % 4, c // 4, r // 2, r % 2]).astype(jnp.int32)
    wide = image.astype(F32)
    up, down = rims(wide[:1], wide[H - 1 :], "row")
    tall = jnp.concatenate([up, wide, down], axis=0)
    left, right = rims(tall[:, :1], tall[:, W - 1 :], "col")
    pix = jnp.concatenate([left, tall, right, jnp.zeros((H + 2, 6, C), F32)], axis=1)
    img = image.reshape(H * W, C)
    cot = cotangent.reshape(H * W, C)
    cw = conv_weight.reshape(9, 1, E)
    cb = conv_bias.reshape(1, E)
    pw = jnp.pad(proj_weight, ((0, 0), (0, 0), (0, 88)))
    dtw = jnp.pad(dt_weight, ((0, 0), (0, 120), (0, 0)))
    entry = lax.broadcasted_iota(jnp.int32, (256, N * 128), 0) & 127
    state = lax.broadcasted_iota(jnp.int32, (256, N * 128), 1) >> 7
    sel = jnp.where(entry == state + 8, 1.0, 0.0).astype(BF16)
    dtb = dt_bias.reshape(4, 1, E)
    alog = a_log.reshape(4 * N, E)
    alog4 = a_log.reshape(4, N, 1, E)
    gain = norm_gain.reshape(1, E)

    tok = ((H * W, E), F32)
    four = (4, H * W, E)
    two = (2, H * W, E)
    rates = (4 * N, 8, E)
    prj = (4, H * W, 128)
    spreads = (2, H * W, N * 128)
    rows = [(2, N, 16, E), (2, 16, E)]
    cols = [(2, N, 8, E), (2, 8, E)]
    mcs = [((2, 9, 16, E), F32)] * 2
    mzs = [((2, 5, 8, E), F32)] * 4
    (rate,) = call(rate_kernel, [alog], [(rates, F32)], [], "rates", 1)
    hid_rc, hid_cr, conv, delta, sig, proj, bb23, *mc = call(
        first_kernel,
        [pos, pix, in_weight, cw, cb, pw, dtw, dtb, rate, sel],
        [tok, tok, tok, (four, F32), (four, F32), (prj, F32), (spreads, F32)] + mcs,
        [(10, 24, E)] + rows, "first", 4,
    )
    bb01, *mz = call(
        col_ends_kernel, [pos, hid_cr, delta, proj, rate, sel], [(spreads, F32)] + mzs, cols,
        "col_ends", 2,
    )
    cc01, cc23, gate = call(
        readout_kernel, [proj, sel, img, in_weight], [(spreads, F32), (spreads, F32), tok], [],
        "readout", 1,
    )
    t, u = exchange(pos, alog4, mz, mc, (0, 1, 2, 3), ((), (cc01,)))
    (y23,) = call(
        row_out_kernel, [pos] + u + [hid_rc, delta, rate, bb23, cc23],
        [tok], rows[:1], "row_out", 3,
    )
    gated, dgate, dtot_rc, dtot_cr, *mc = call(
        middle_kernel,
        [pos] + t + [hid_rc, hid_cr, gate, delta, rate, bb01, cc01, cc23, y23, skip_gain, gain,
                     out_weight, cot],
        [tok, tok, tok, tok] + mcs,
        [tok[0]] + cols[:1] + rows, "middle", 5,
    )
    mz = call(
        col_back_kernel, [pos, delta, dtot_cr, rate, cc01], mzs, cols, "col_back", 2
    )
    out, g_out, g_gate, gate_pix = call(
        side_kernel, [gated, dgate, out_weight, cot, img, in_weight],
        [((H * W, C), BF16), ((E, C), F32), ((C, E), F32), ((H * W, C), F32)], [], "side", 1,
    )
    dpcs = ((2, H * W, 128), F32)
    hist01, dpc01 = call(
        replay_kernel, [pos] + t + [hid_cr, delta, rate, bb01, dtot_cr, sel],
        [((2, W, N, 8, E), F32), dpcs], cols[:1] + [spreads], "replay", 2,
    )
    hist23, dpc23 = call(
        row_replay_kernel, [pos] + u + [hid_rc, delta, rate, bb23, dtot_rc, sel],
        [((4, H, N, 8, E), F32), dpcs], rows[:1] + [spreads], "row_replay", 2,
    )
    b, v = exchange(pos, alog4, mz, mc, (1, 0, 3, 2), ((hist23, g_out), (hist01,)))
    work = [(2 * N, 8, E), tok[0], spreads, two]
    drc, g_a23 = call(
        row_grad_kernel,
        [pos] + v + [hist23, dpc23, hid_rc, delta, sig, rate, bb23, cc23, dtot_rc, skip_gain, pw, dtw,
                     alog, sel],
        [tok, ((2 * N, E), F32)],
        [rows[0]] + work, "row_grad", 7,
    )
    msg, center = call(
        last_kernel,
        [pos] + b + [hist01, dpc01, hid_cr, conv, delta, sig, rate, bb01, cc01, dtot_cr, drc, g_a23,
                     alog, skip_gain, pw, dtw, cw, in_weight, pix, g_out, g_gate, gate_pix, sel],
        [((1024, 128), F32), ((H * W, C), F32)],
        work + [cols[0], (12, 32, E), (10, 24, C), (128, 128)],
        "last", 8,
    )
    got = lax.all_to_all(msg.reshape(128, 8, 128), AXES, 0, 0, tiled=True)
    (back,) = call(sum_kernel, [got.reshape(1024, 128)], [((1024, 128), F32)], [], "sum")
    got = lax.all_to_all(back.reshape(128, 8, 128), AXES, 0, 0, tiled=True)
    g_pix, g_in, g_outw, g_a = call(
        finish_kernel, [got.reshape(1024, 128), center],
        [((H * W, C), BF16), ((C, 2 * E), F32), ((E, C), F32), ((4 * N, E), F32)],
        [(H, W, C)], "finish",
    )
    return (
        out.reshape(H, W, C), g_pix.reshape(H, W, C), g_in, g_outw, g_a.reshape(4, N, E),
    )


def solution(mesh):
    tile = P("row", "col", None)
    return jax.shard_map(
        per_device,
        mesh=mesh,
        in_specs=(tile,) + (P(),) * 10 + (tile,),
        out_specs=(tile, tile, P(), P(), P()),
        check_vma=False,
    )
```

```python
from functools import partial

import jax
import jax.numpy as jnp
from jax import lax
from jax.experimental import pallas as pl
from jax.experimental.pallas import tpu as pltpu
from jax.sharding import PartitionSpec as P

F32 = jnp.float32
BF16 = jnp.bfloat16
H, W, C, E, N = 8, 16, 128, 256, 16
LOG2E = 1.4426950408889634
LN2 = 0.6931471805599453
AXES = ("row", "col")


def split2(a):
    hi = a.astype(BF16)
    return hi, (a - hi.astype(F32)).astype(BF16)


def dot(a, b, dims):
    return lax.dot_general(a, b, (dims, ((), ())), preferred_element_type=F32)


NN = ((1,), (0,))
NT = ((1,), (1,))


def mm3(a, b, dims=NN):
    ah, al = split2(a)
    bh, bl = split2(b)
    return dot(ah, bh, dims) + (dot(ah, bl, dims) + dot(al, bh, dims))


def mm2(a, b, dims=NN):
    ah, al = split2(a)
    return dot(ah, b, dims) + dot(al, b, dims)


def mm2r(a, b, dims=NN):
    bh, bl = split2(b)
    return dot(a, bh, dims) + dot(a, bl, dims)


def permute_tokens(x, to_cr):
    o = lax.broadcasted_iota(jnp.int32, (128, 128), 0)
    i = lax.broadcasted_iota(jnp.int32, (128, 128), 1)
    if to_cr:
        hit = i == ((o & 7) * 16 + (o >> 3))
    else:
        hit = i == ((o & 15) * 8 + (o >> 4))
    m = jnp.where(hit, 1.0, 0.0).astype(BF16)
    hi = x.astype(BF16)
    rest = x - hi.astype(F32)
    mid = rest.astype(BF16)
    low = (rest - mid.astype(F32)).astype(BF16)
    return dot(m, hi, NN) + (dot(m, mid, NN) + dot(m, low, NN))


def softplus(z):
    return jnp.maximum(z, 0.0) + jnp.log1p(jnp.exp(-jnp.abs(z)))


def sigmoid(v):
    return 1.0 / (1.0 + jnp.exp(-v))


def spread(p, sel, dst):
    hi, lo = split2(p)
    dst[...] = dot(jnp.concatenate([hi, lo], axis=1), sel[...], NN)


def lanes(ref, k, at, n):
    v = ref[k, at, 128 * n : 128 * n + 128]
    return jnp.concatenate([v, v], axis=1)


def fold(v):
    return v[:, :128] + v[:, 128:]


def fill_rates(alog, rate):
    r = -jnp.exp(alog[...]) * LOG2E
    for i in range(4 * N):
        rate[i] = jnp.broadcast_to(r[i : i + 1], (8, E))


def steps(k):
    return W if k < 2 else H


def groups(k):
    return (0,) if k < 2 else (0, 1)


def row_at(k, g, i):
    t = i if k % 2 == 0 else steps(k) - 1 - i
    start = t * 8 if k < 2 else t * 16 + g * 8
    return pl.multiple_of(start, 8)


def end_states(k, g, delta, h, rate, bb):
    def body(i, s):
        at = pl.ds(row_at(k, g, i), 8)
        d = delta[k, at, :]
        u = d * h[at, :]
        new = [
            jnp.exp2(d * rate[k * N + n]) * s[n] + u * lanes(bb, k % 2, at, n) for n in range(N)
        ]
        return tuple(new) + (s[N] + d,)

    return lax.fori_loop(0, steps(k), body, (jnp.zeros((8, E), F32),) * (N + 1), unroll=2)


def outputs(k, g, start, delta, h, rate, bb, cc, yy):
    def body(i, s):
        at = pl.ds(row_at(k, g, i), 8)
        d = delta[k, at, :]
        u = d * h[at, :]
        y = None
        new = []
        for n in range(N):
            v = jnp.exp2(d * rate[k * N + n]) * s[n] + u * lanes(bb, k % 2, at, n)
            new.append(v)
            c = v * lanes(cc, k % 2, at, n)
            y = c if y is None else y + c
        yy[at, :] = y if k % 2 == 0 else yy[at, :] + y
        return tuple(new)

    lax.fori_loop(0, steps(k), body, start, unroll=2)


def end_adjoints(k, g, delta, dy, rate, cc):
    def body(j, s):
        at = pl.ds(row_at(k, g, steps(k) - 1 - j), 8)
        d = delta[k, at, :]
        t = dy[at, :]
        new = [
            jnp.exp2(d * rate[k * N + n]) * (s[n] + t * lanes(cc, k % 2, at, n))
            for n in range(N)
        ]
        return tuple(new) + (s[N] + d,)

    return lax.fori_loop(0, steps(k), body, (jnp.zeros((8, E), F32),) * (N + 1), unroll=2)


def history(k, g, start, delta, h, rate, bb, hist, dy, xc):
    def body(i, s):
        at = pl.ds(row_at(k, g, i), 8)
        d = delta[k, at, :]
        u = d * h[at, :]
        t = dy[at, :]
        new = []
        for n in range(N):
            hist[i, n] = s[n]
            v = jnp.exp2(d * rate[k * N + n]) * s[n] + u * lanes(bb, k % 2, at, n)
            new.append(v)
            xc[k % 2, at, 128 * n : 128 * n + 128] = fold(t * v)
        return tuple(new)

    lax.fori_loop(0, steps(k), body, start, unroll=2)


def readout_gradient(xc, sel, dpc):
    for kk in range(2):
        dpc[kk] = pltpu.roll(mm2(xc[kk], sel[0:128, :], NT), N, 1)


def gradients(k, g, end, delta, sig, h, dy, rate, bb, cc, hist, skip, xb, dz, dx, drate):
    kk = k % 2

    def body(j, m):
        i = steps(k) - 1 - j
        at = pl.ds(row_at(k, g, i), 8)
        d = delta[k, at, :]
        xx = h[at, :]
        u = d * xx
        t = dy[at, :]
        du = jnp.zeros((8, E), F32)
        dd = jnp.zeros((8, E), F32)
        new = []
        for n in range(N):
            r = rate[k * N + n]
            lam = lanes(cc, kk, at, n) * t + m[n]
            out = jnp.exp2(d * r) * lam
            new.append(out)
            xb[kk, at, 128 * n : 128 * n + 128] = fold(lam * u)
            du = du + lam * lanes(bb, kk, at, n)
            q = out * hist[i, n]
            dd = dd + q * r
            drate[kk * N + n] = drate[kk * N + n] + q * d
        dz[kk, at, :] = (du * xx + dd * LN2) * sig[k, at, :]
        dxv = du * d + skip[k : k + 1] * t
        dx[at, :] = dxv if kk == 0 else dx[at, :] + dxv
        return tuple(new)

    lax.fori_loop(0, steps(k), body, end)


def close_pair(first, dx, dz, xb, dpc, dtw, pw, sel):
    total = dx[...]
    pick = sel[0:128, :]
    for kk in range(2):
        dp = (
            mm3(dz[kk], dtw[first + kk], NT) + mm2(xb[kk], pick, NT) + dpc[kk]
        )
        total = total + mm3(dp, pw[first + kk], NT)
    return total


def rate_gradient(drate, alog, first):
    return jnp.sum(drate[...], axis=1) * (-jnp.exp(alog[N * first : N * first + 2 * N]))


def keep_col(f, s, col_f, col_d):
    for n in range(N):
        col_f[f, n] = s[n]
    col_d[f] = s[N]


def col_message(pos, col_f, col_d, mz):
    for d in range(4):
        q = jnp.bitwise_xor(pos[0], d)
        for f in range(2):
            mz[d][f, 0:4] = col_f[f, pl.ds(4 * q, 4)]
            mz[d][f, 4] = col_d[f]


def place_cols(pos, t, col_s):
    for d in range(4):
        q = jnp.bitwise_xor(pos[0], d)
        for f in range(2):
            col_s[f, pl.ds(4 * q, 4)] = t[d][f]


def col_start(col_s, f):
    return tuple(col_s[f, n] for n in range(N))


def keep_row(f, g, s, row_f, row_d):
    for n in range(N):
        row_f[f, n, 8 * g : 8 * g + 8, :] = s[n]
    row_d[f, 8 * g : 8 * g + 8, :] = s[N]


def row_message(pos, row_f, row_d, mc):
    for d in range(2):
        h = jnp.bitwise_xor(pos[3], d)
        for f in range(2):
            mc[d][f, 0:8] = row_f[f, pl.ds(8 * h, 8)]
            mc[d][f, 8] = row_d[f]


def place_rows(pos, u, row_s):
    for d in range(2):
        h = jnp.bitwise_xor(pos[3], d)
        for f in range(2):
            row_s[f, pl.ds(8 * h, 8)] = u[d][f]


def row_start(row_s, f, g):
    return tuple(row_s[f, n, 8 * g : 8 * g + 8, :] for n in range(N))


def first_kernel(
    pos, pix, win, cw, cb, pw, dtw, dtb, rate, sel,
    hid_rc, hid_cr, conv, delta, sig, proj, bb, mc0, mc1,
    mix, row_f, row_d,
):
    x = pix[...].reshape(10 * 24, C).astype(BF16)
    mix[...] = dot(x, win[:, :E], NN).reshape(10, 24, E)
    acc = jnp.broadcast_to(cb[...].reshape(1, 1, E), (H, W, E))
    for j in range(3):
        for i in range(3):
            acc = acc + mix[i : i + H, j : j + W, :] * cw[3 * i + j].reshape(1, 1, E)
    acc = acc.reshape(H * W, E)
    conv[...] = acc
    hid = acc * sigmoid(acc)
    hid_rc[...] = hid
    cr = permute_tokens(hid, True)
    hid_cr[...] = cr
    for k in range(4):
        pk = mm3(cr if k < 2 else hid, pw[k])
        proj[k] = pk
        if k >= 2:
            spread(pk, sel, bb.at[k - 2])
        zk = mm3(pk, dtw[k]) + dtb[k]
        sig[k] = sigmoid(zk)
        delta[k] = softplus(zk)
    for k in (2, 3):
        for g in (0, 1):
            keep_row(k - 2, g, end_states(k, g, delta, hid_rc, rate, bb), row_f, row_d)
    row_message(pos, row_f, row_d, (mc0, mc1))


def rate_kernel(alog, rate):
    fill_rates(alog, rate)


def col_ends_kernel(
    pos, hid_cr, delta, proj, rate, sel, bb, mz0, mz1, mz2, mz3, col_f, col_d
):
    for k in range(2):
        spread(proj[k], sel, bb.at[k])
    for k in range(2):
        keep_col(k, end_states(k, 0, delta, hid_cr, rate, bb), col_f, col_d)
    col_message(pos, col_f, col_d, (mz0, mz1, mz2, mz3))


def readout_kernel(proj, sel, img, win, cc01, cc23, gate):
    for k in range(4):
        cc = cc01 if k < 2 else cc23
        spread(pltpu.roll(proj[k], 128 - N, 1), sel, cc.at[k % 2])
    gate[...] = dot(img[...], win[:, E:], NN)


def decay(alog, k, n, d):
    r = -jnp.exp(alog[k, n]) * LOG2E
    return jnp.exp2(d * jnp.broadcast_to(r, d.shape))


def row_join_kernel(ks, pos, alog, c0, c1, gy, rc):
    core = pos[3]
    for d, r in enumerate((c0, c1)):
        rc[jnp.bitwise_xor(core, d)] = r[...]
    for f in range(2):
        one, two = (0, 1) if f == 0 else (1, 0)
        for n in range(8):
            gy[f, n] = (
                rc[one, f, n] * decay(alog, ks[2 + f], 8 * core + n, rc[two, f, 8])
                + rc[two, f, n]
            )
        gy[f, 8] = rc[0, f, 8] + rc[1, f, 8]


def join_kernel(ks, pos, alog, r0, r1, r2, r3, g0, g1, mx1, mx2, mx3, my, rs, gx):
    z, x, y, core = pos[0], pos[1], pos[2], pos[3]
    for d, r in enumerate((r0, r1, r2, r3)):
        rs[jnp.bitwise_xor(z, d)] = r[...]
    for f in range(2):
        order = range(4) if f == 0 else range(3, -1, -1)
        for n in range(4):
            total = None
            for t in order:
                piece = rs[t, f, n]
                total = piece if total is None else (
                    total * decay(alog, ks[f], 4 * z + n, rs[t, f, 4]) + piece
                )
            gx[f, n] = total
        gx[f, 4] = rs[0, f, 4] + rs[1, f, 4] + rs[2, f, 4] + rs[3, f, 4]
    for d, m in ((1, mx1), (2, mx2), (3, mx3)):
        m[...] = gx[jnp.where(jnp.bitwise_xor(x, d) > x, 0, 1)]
    f = y >> 1
    mine_first = (y & 1) == f
    own, other = g0[f], g1[f]
    k = jnp.where(f == 0, ks[2], ks[3])
    late = jnp.where(mine_first, other[8], own[8])
    for n in range(8):
        head = jnp.where(mine_first, own[n], other[n])
        tail = jnp.where(mine_first, other[n], own[n])
        my[n] = head * decay(alog, k, 8 * core + n, late) + tail


def start_kernel(
    ks, pos, alog, r0, r1, r2, r3, c0, c1, x1, x2, x3, g1, g2,
    so0, so1, so2, so3, co0, co1, rs, rc, xs, oz, oc,
):
    z, x, y, core = pos[0], pos[1], pos[2], pos[3]
    for d, r in enumerate((r0, r1, r2, r3)):
        rs[jnp.bitwise_xor(z, d)] = r[...]
    for d, r in enumerate((c0, c1)):
        rc[jnp.bitwise_xor(core, d)] = r[...]
    xs[x] = jnp.zeros((5, 8, E), F32)
    for d, r in ((1, x1), (2, x2), (3, x3)):
        xs[jnp.bitwise_xor(x, d)] = r[...]
    for f in range(2):
        order = list(range(4)) if f == 0 else list(range(3, -1, -1))
        for n in range(4):
            s = jnp.zeros((8, E), F32)
            for p in order:
                before = p < x if f == 0 else p > x
                new = s * decay(alog, ks[f], 4 * z + n, xs[p, 4]) + xs[p, n]
                s = jnp.where(before, new, s)
            for t in order:
                oz[t, f, n] = s
                if t != order[-1]:
                    s = s * decay(alog, ks[f], 4 * z + n, rs[t, f, 4]) + rs[t, f, n]
        one, two = (0, 1) if f == 0 else (1, 0)
        far = (y >> 1) == 1 - f
        near = (y & 1) == 1 - f
        for n in range(8):
            s = jnp.where(far, g2[n], 0.0)
            new = s * decay(alog, ks[2 + f], 8 * core + n, g1[f, 8]) + g1[f, n]
            s = jnp.where(near, new, s)
            oc[one, f, n] = s
            oc[two, f, n] = (
                s * decay(alog, ks[2 + f], 8 * core + n, rc[one, f, 8]) + rc[one, f, n]
            )
    for d, o in enumerate((so0, so1, so2, so3)):
        o[...] = oz[jnp.bitwise_xor(z, d)]
    for d, o in enumerate((co0, co1)):
        o[...] = oc[jnp.bitwise_xor(core, d)]


def row_out_kernel(
    pos, u0, u1, hid_rc, delta, rate, bb, cc, yy, row_s,
):
    place_rows(pos, (u0, u1), row_s)
    for k in (2, 3):
        for g in (0, 1):
            outputs(k, g, row_start(row_s, k - 2, g), delta, hid_rc, rate, bb, cc, yy)


def middle_kernel(
    pos, t0, t1, t2, t3, hid_rc, hid_cr, gate, delta, rate, bb, cc, cc23, y23, skip, gain, ow,
    cot,
    gated_out, dgate_out, dtot_rc, dtot_cr, mc0, mc1,
    y01, col_s, row_f, row_d,
):
    place_cols(pos, (t0, t1, t2, t3), col_s)
    for k in range(2):
        outputs(k, 0, col_start(col_s, k), delta, hid_cr, rate, bb, cc, y01)
    skips = skip[0:1] + skip[1:2] + skip[2:3] + skip[3:4]
    total = y23[...] + permute_tokens(y01[...], False) + skips * hid_rc[...]
    centered = total - jnp.mean(total, axis=-1, keepdims=True)
    inv = lax.rsqrt(jnp.mean(centered * centered, axis=-1, keepdims=True) + 1e-05)
    unit = centered * inv
    normed = unit * gain[...]
    gv = gate[...]
    sg = sigmoid(gv)
    act = gv * sg
    gated_out[...] = normed * act
    dgated = dot(cot[...], ow[...], NT)
    dgate_out[...] = dgated * normed * (sg * (1.0 + gv * (1.0 - sg)))
    dn = dgated * act * gain[...]
    dt = inv * (
        dn
        - jnp.mean(dn, axis=-1, keepdims=True)
        - unit * jnp.mean(dn * unit, axis=-1, keepdims=True)
    )
    dtot_rc[...] = dt
    dtot_cr[...] = permute_tokens(dt, True)
    for k in (2, 3):
        for g in (0, 1):
            keep_row(3 - k, g, end_adjoints(k, g, delta, dtot_rc, rate, cc23), row_f, row_d)
    row_message(pos, row_f, row_d, (mc0, mc1))


def side_kernel(gated, dgate, ow, cot, img, win, out, g_out, g_gate, gate_pix):
    gv = gated[...]
    out[...] = mm2(gv, ow[...]).astype(BF16)
    g_out[...] = mm2(gv.T, cot[...])
    dg = dgate[...]
    g_gate[...] = mm2r(img[...].astype(F32).T.astype(BF16), dg)
    gate_pix[...] = mm2(dg, win[:, E:], NT)


def replay_kernel(
    pos, t0, t1, t2, t3, hid_cr, delta, rate, bb, dy, sel, hist, dpc, col_s, xc
):
    place_cols(pos, (t0, t1, t2, t3), col_s)
    for k in range(2):
        history(k, 0, col_start(col_s, k), delta, hid_cr, rate, bb, hist.at[k], dy, xc)
    readout_gradient(xc, sel, dpc)


def row_replay_kernel(pos, u0, u1, hid_rc, delta, rate, bb, dy, sel, hist, dpc, row_s, xc):
    place_rows(pos, (u0, u1), row_s)
    for k in (2, 3):
        for g in (0, 1):
            history(
                k, g, row_start(row_s, k - 2, g), delta, hid_rc, rate, bb,
                hist.at[2 * (k - 2) + g], dy, xc,
            )
    readout_gradient(xc, sel, dpc)


def col_back_kernel(pos, delta, dtot_cr, rate, cc, mz0, mz1, mz2, mz3, col_f, col_d):
    for k in range(2):
        keep_col(1 - k, end_adjoints(k, 0, delta, dtot_cr, rate, cc), col_f, col_d)
    col_message(pos, col_f, col_d, (mz0, mz1, mz2, mz3))


def row_grad_kernel(
    pos, v0, v1, hist, dpc, hid_rc, delta, sig, rate, bb, cc, dtot_rc, skip, pw, dtw, alog, sel,
    drc, g_a,
    row_b, drate, dx, xb, dz,
):
    place_rows(pos, (v0, v1), row_b)
    drate[...] = jnp.zeros_like(drate)
    for k in (2, 3):
        for g in (0, 1):
            gradients(
                k, g, row_start(row_b, 3 - k, g), delta, sig, hid_rc, dtot_rc, rate, bb, cc,
                hist.at[2 * (k - 2) + g], skip, xb, dz, dx, drate,
            )
    g_a[...] = rate_gradient(drate, alog, 2)
    drc[...] = close_pair(2, dx, dz, xb, dpc, dtw, pw, sel)


def last_kernel(
    pos, b0, b1, b2, b3, hist, dpc, hid_cr, conv, delta, sig, rate, bb, cc, dtot_cr, drc,
    g_a23, alog, skip, pw, dtw, cw, win, pix, g_out, g_gate, gate_pix, sel,
    msg, center,
    drate, dx, xb, dz, col_b, zpad, gp, edge,
):
    place_cols(pos, (b0, b1, b2, b3), col_b)
    drate[...] = jnp.zeros_like(drate)
    for k in range(2):
        gradients(
            k, 0, col_start(col_b, 1 - k), delta, sig, hid_cr, dtot_cr, rate, bb, cc,
            hist.at[k], skip, xb, dz, dx, drate,
        )
    g_a = jnp.concatenate([rate_gradient(drate, alog, 0), g_a23[...]], axis=0)
    dcr = close_pair(0, dx, dz, xb, dpc, dtw, pw, sel)
    dhid = drc[...] + permute_tokens(dcr, False)
    cv = conv[...]
    sg = sigmoid(cv)
    dconv = dhid * (sg * (1.0 + cv * (1.0 - sg)))
    zpad[...] = jnp.zeros_like(zpad)
    zpad[2:10, 8:24, :] = dconv.reshape(H, W, E)
    acc = jnp.zeros((10, 24, E), F32)
    for j in range(3):
        for i in range(3):
            acc = acc + zpad[2 - i : 12 - i, 8 - j : 32 - j, :] * cw[3 * i + j].reshape(1, 1, E)
    flat = acc.reshape(240, E)
    gp[...] = mm2(flat, win[:, :E], NT).reshape(10, 24, C)
    pt = pix[...].reshape(240, C)
    g_in = mm2r(pt.T.astype(BF16), flat)
    center[...] = gate_pix[...] + gp[1:9, 1:17, :].reshape(128, C)
    edge[...] = jnp.zeros_like(edge)
    edge[0:16] = gp[9, 1:17, :]
    edge[16:32] = gp[0, 1:17, :]
    edge[32:40] = gp[1:9, 17, :]
    edge[40:48] = gp[1:9, 0, :]
    edge[48:49] = gp[9, 17:18, :]
    edge[49:50] = gp[9, 0:1, :]
    edge[50:51] = gp[0, 17:18, :]
    edge[51:52] = gp[0, 0:1, :]
    blocks = (
        g_in[:, :128],
        g_in[:, 128:],
        g_gate[:, :128],
        g_gate[:, 128:],
        g_out[:128],
        g_out[128:],
        jnp.concatenate([g_a[:, :128], g_a[:, 128:]], axis=0),
        edge[...].T,
    )
    for b, block in enumerate(blocks):
        msg[pl.ds(b, 128, stride=8), :] = block


def sum_kernel(r, o):
    s = jnp.sum(r[...].reshape(128, 8, 128), axis=0)
    h = r[pl.ds(7, 128, stride=8), :]
    d = lax.broadcasted_iota(jnp.int32, (128, 128), 0)
    i = lax.broadcasted_iota(jnp.int32, (128, 128), 1)
    rr, cc = d >> 4, d & 15
    inn = jnp.zeros((128, 128), F32)
    for lo, hi, dr, dc in (
        (0, 16, -1, 0), (16, 32, 1, 0), (32, 40, 0, -1), (40, 48, 0, 1),
        (48, 49, -1, -1), (49, 50, -1, 1), (50, 51, 1, -1), (51, 52, 1, 1),
    ):
        moved = pltpu.roll(h, (-(dr * 16 + dc)) % 128, 0)
        ok = (i >= lo) & (i < hi)
        ok = ok & (rr + dr >= 0) & (rr + dr < 8) & (cc + dc >= 0) & (cc + dc < 16)
        inn = jnp.where(ok, moved, inn)
    o[...] = jnp.broadcast_to(s[None], (128, 8, 128)).reshape(1024, 128)
    o[pl.ds(7, 128, stride=8), :] = inn


def finish_kernel(q, center, g_pix, g_in, g_out, g_a, acc):
    def block(b):
        return q[pl.ds(b, 128, stride=8), :]

    for b in range(4):
        g_in[:, 128 * b : 128 * b + 128] = block(b)
    g_out[:128] = block(4)
    g_out[128:] = block(5)
    a = block(6)
    g_a[:, :128] = a[:64]
    g_a[:, 128:] = a[64:]
    inn = block(7).T
    acc[...] = center[...].reshape(H, W, C)
    acc[0] = acc[0] + inn[0:16]
    acc[7] = acc[7] + inn[16:32]
    acc[:, 0, :] = acc[:, 0, :] + inn[32:40]
    acc[:, 15, :] = acc[:, 15, :] + inn[40:48]
    acc[0, 0:1, :] = acc[0, 0:1, :] + inn[48:49]
    acc[0, 15:16, :] = acc[0, 15:16, :] + inn[49:50]
    acc[7, 0:1, :] = acc[7, 0:1, :] + inn[50:51]
    acc[7, 15:16, :] = acc[7, 15:16, :] + inn[51:52]
    g_pix[...] = acc[...].reshape(H * W, C).astype(BF16)


def call(kernel, ins, outs, scratch, name, cost=1, after=()):
    vmem = pl.BlockSpec(memory_space=pltpu.VMEM)
    specs = [
        pl.BlockSpec(memory_space=pltpu.SMEM) if x.dtype == jnp.int32 else vmem for x in ins
    ]
    used, extra = len(ins), len(after)

    def body(*refs):
        kernel(*refs[:used], *refs[used + extra :])

    return pl.pallas_call(
        body,
        out_shape=[jax.ShapeDtypeStruct(s, t) for s, t in outs],
        in_specs=specs + [pl.BlockSpec(memory_space=pl.ANY)] * extra,
        out_specs=[vmem] * len(outs),
        scratch_shapes=[pltpu.VMEM(s, F32) for s in scratch],
        compiler_params=pltpu.CompilerParams(vmem_limit_bytes=14 * 1024 * 1024),
        cost_estimate=pl.CostEstimate(
            flops=0, bytes_accessed=cost * 3_500_000, transcendentals=0
        ),
        name=name,
    )(*ins, *after)


def xor_permute(x, axis, mask):
    return lax.ppermute(x, axis, [(i, i ^ mask) for i in range(lax.axis_size(axis))])


def exchange(pos, alog4, mz, mc, ks, after=((), ())):
    r = [mz[0]] + [xor_permute(mz[d], "col", d) for d in range(1, 4)]
    c = [mc[0], xor_permute(mc[1], "row", 1)]
    (g0,) = call(
        partial(row_join_kernel, ks), [pos, alog4] + c, [((2, 9, 16, E), F32)],
        [(2, 2, 9, 16, E)], "row_join", 1, (mz[0],),
    )
    g1 = xor_permute(g0, "row", 2)
    m = call(
        partial(join_kernel, ks), [pos, alog4] + r + [g0, g1],
        [((5, 8, E), F32)] * 3 + [((8, 16, E), F32)],
        [(4, 2, 5, 8, E), (2, 5, 8, E)], "join", 1, after[0],
    )
    g2 = xor_permute(m[3], "row", 4)
    xm = [xor_permute(m[d - 1], "col", 4 * d) for d in range(1, 4)]
    s = call(
        partial(start_kernel, ks), [pos, alog4] + r + c + xm + [g1, g2],
        [((2, 4, 8, E), F32)] * 4 + [((2, 8, 16, E), F32)] * 2,
        [(4, 2, 5, 8, E), (2, 2, 9, 16, E), (4, 5, 8, E), (4, 2, 4, 8, E), (2, 2, 8, 16, E)],
        "starts", 1, after[1],
    )
    t = [s[0]] + [xor_permute(s[d], "col", d) for d in range(1, 4)]
    u = [s[4], xor_permute(s[5], "row", 1)]
    return t, u


def rims(head, tail, axis):
    count = lax.axis_size(axis)
    mine = lax.axis_index(axis)
    odd = mine % 2 == 1
    near = xor_permute(jnp.where(odd, head, tail), axis, 1)
    pairs = [(i, (i + 1 if i % 2 == 1 else i - 1) % count) for i in range(count)]
    far = lax.ppermute(jnp.where(odd, tail, head), axis, pairs)
    before = jnp.where(mine == 0, 0.0, jnp.where(odd, near, far))
    after = jnp.where(mine == count - 1, 0.0, jnp.where(odd, far, near))
    return before, after


def per_device(
    image, in_weight, conv_weight, conv_bias, proj_weight, dt_weight, dt_bias, a_log,
    skip_gain, norm_gain, out_weight, cotangent,
):
    r, c = lax.axis_index("row"), lax.axis_index("col")
    pos = jnp.stack([c % 4, c // 4, r // 2, r % 2]).astype(jnp.int32)
    wide = image.astype(F32)
    up, down = rims(wide[:1], wide[H - 1 :], "row")
    tall = jnp.concatenate([up, wide, down], axis=0)
    left, right = rims(tall[:, :1], tall[:, W - 1 :], "col")
    pix = jnp.concatenate([left, tall, right, jnp.zeros((H + 2, 6, C), F32)], axis=1)
    img = image.reshape(H * W, C)
    cot = cotangent.reshape(H * W, C)
    cw = conv_weight.reshape(9, 1, E)
    cb = conv_bias.reshape(1, E)
    pw = jnp.pad(proj_weight, ((0, 0), (0, 0), (0, 88)))
    dtw = jnp.pad(dt_weight, ((0, 0), (0, 120), (0, 0)))
    entry = lax.broadcasted_iota(jnp.int32, (256, N * 128), 0) & 127
    state = lax.broadcasted_iota(jnp.int32, (256, N * 128), 1) >> 7
    sel = jnp.where(entry == state + 8, 1.0, 0.0).astype(BF16)
    dtb = dt_bias.reshape(4, 1, E)
    alog = a_log.reshape(4 * N, E)
    alog4 = a_log.reshape(4, N, 1, E)
    gain = norm_gain.reshape(1, E)

    tok = ((H * W, E), F32)
    four = (4, H * W, E)
    two = (2, H * W, E)
    rates = (4 * N, 8, E)
    prj = (4, H * W, 128)
    spreads = (2, H * W, N * 128)
    rows = [(2, N, 16, E), (2, 16, E)]
    cols = [(2, N, 8, E), (2, 8, E)]
    mcs = [((2, 9, 16, E), F32)] * 2
    mzs = [((2, 5, 8, E), F32)] * 4
    (rate,) = call(rate_kernel, [alog], [(rates, F32)], [], "rates", 1)
    hid_rc, hid_cr, conv, delta, sig, proj, bb23, *mc = call(
        first_kernel,
        [pos, pix, in_weight, cw, cb, pw, dtw, dtb, rate, sel],
        [tok, tok, tok, (four, F32), (four, F32), (prj, F32), (spreads, F32)] + mcs,
        [(10, 24, E)] + rows, "first", 4,
    )
    bb01, *mz = call(
        col_ends_kernel, [pos, hid_cr, delta, proj, rate, sel], [(spreads, F32)] + mzs, cols,
        "col_ends", 2,
    )
    cc01, cc23, gate = call(
        readout_kernel, [proj, sel, img, in_weight], [(spreads, F32), (spreads, F32), tok], [],
        "readout", 1,
    )
    t, u = exchange(pos, alog4, mz, mc, (0, 1, 2, 3), ((), (cc01,)))
    (y23,) = call(
        row_out_kernel, [pos] + u + [hid_rc, delta, rate, bb23, cc23],
        [tok], rows[:1], "row_out", 3,
    )
    gated, dgate, dtot_rc, dtot_cr, *mc = call(
        middle_kernel,
        [pos] + t + [hid_rc, hid_cr, gate, delta, rate, bb01, cc01, cc23, y23, skip_gain, gain,
                     out_weight, cot],
        [tok, tok, tok, tok] + mcs,
        [tok[0]] + cols[:1] + rows, "middle", 5,
    )
    mz = call(
        col_back_kernel, [pos, delta, dtot_cr, rate, cc01], mzs, cols, "col_back", 2
    )
    out, g_out, g_gate, gate_pix = call(
        side_kernel, [gated, dgate, out_weight, cot, img, in_weight],
        [((H * W, C), BF16), ((E, C), F32), ((C, E), F32), ((H * W, C), F32)], [], "side", 1,
    )
    dpcs = ((2, H * W, 128), F32)
    hist01, dpc01 = call(
        replay_kernel, [pos] + t + [hid_cr, delta, rate, bb01, dtot_cr, sel],
        [((2, W, N, 8, E), F32), dpcs], cols[:1] + [spreads], "replay", 2,
    )
    hist23, dpc23 = call(
        row_replay_kernel, [pos] + u + [hid_rc, delta, rate, bb23, dtot_rc, sel],
        [((4, H, N, 8, E), F32), dpcs], rows[:1] + [spreads], "row_replay", 2,
    )
    b, v = exchange(pos, alog4, mz, mc, (1, 0, 3, 2), ((hist23, g_out), (hist01,)))
    work = [(2 * N, 8, E), tok[0], spreads, two]
    drc, g_a23 = call(
        row_grad_kernel,
        [pos] + v + [hist23, dpc23, hid_rc, delta, sig, rate, bb23, cc23, dtot_rc, skip_gain, pw, dtw,
                     alog, sel],
        [tok, ((2 * N, E), F32)],
        [rows[0]] + work, "row_grad", 7,
    )
    msg, center = call(
        last_kernel,
        [pos] + b + [hist01, dpc01, hid_cr, conv, delta, sig, rate, bb01, cc01, dtot_cr, drc, g_a23,
                     alog, skip_gain, pw, dtw, cw, in_weight, pix, g_out, g_gate, gate_pix, sel],
        [((1024, 128), F32), ((H * W, C), F32)],
        work + [cols[0], (12, 32, E), (10, 24, C), (128, 128)],
        "last", 8,
    )
    got = lax.all_to_all(msg.reshape(128, 8, 128), AXES, 0, 0, tiled=True)
    (back,) = call(sum_kernel, [got.reshape(1024, 128)], [((1024, 128), F32)], [], "sum")
    got = lax.all_to_all(back.reshape(128, 8, 128), AXES, 0, 0, tiled=True)
    g_pix, g_in, g_outw, g_a = call(
        finish_kernel, [got.reshape(1024, 128), center],
        [((H * W, C), BF16), ((C, 2 * E), F32), ((E, C), F32), ((4 * N, E), F32)],
        [(H, W, C)], "finish",
    )
    return (
        out.reshape(H, W, C), g_pix.reshape(H, W, C), g_in, g_outw, g_a.reshape(4, N, E),
    )


def solution(mesh):
    tile = P("row", "col", None)
    return jax.shard_map(
        per_device,
        mesh=mesh,
        in_specs=(tile,) + (P(),) * 10 + (tile,),
        out_specs=(tile, tile, P(), P(), P()),
        check_vma=False,
    )
```
